32 devices in a mesh: row: 4 (over y, core), col: 8 (over z, x).
Axes of the slice: x: 2, y: 2, z: 4, core: 2. Of those that a mesh axis runs over, the one named last changes fastest.
Arguments:
- left_values: bfloat16 [4096, 1024], P('col', 'row'), may hold values from 0.1 to 18, as said below
- left_pattern: int32 [32, 8], replicated, may hold values from 0 to 1, as said below
- right_values: bfloat16 [1024, 4096], P('col', 'row'), may hold values from 0.099609375 to 1
- right_pattern: int32 [8, 32], replicated, may hold values from 0 to 1, as said below
Outputs:
- flow: float32 [4096, 4096], P('col', 'row')
The draws below stay inside these ranges and needn't reach their ends.
Inputs may be any that keep to these rules, and one draw needn't show every extreme that they name: left_pattern[i, i % 8] is 1 for every block row i; in every block row, each aligned group of 2 block columns holds at most 1 ones, and some group holds exactly 1. right_pattern[j % 8, j] is 1 for every block column j; in every block row, each aligned group of 8 block columns holds at most 4 ones, and some group holds exactly 4. `left_values`: positive entries.
All inputs are finite; a program needn't handle non-finite values.
Results may differ from the reference program's by a relative error of at most 0.0003.
Values may be sent and summed in bfloat16 or wider, within the bound.
A program may use at most 64 MiB of HBM per device.

```python
import math
import jax
import jax.numpy as jnp

COL_BLOCKS = 8
SLOTS = 4
BLOCK_ROWS = 32
BLOCK_INNER = 8
BLOCK_COLS = 32
LEFT_GROUP = 2
LEFT_SLOTS = 1
ROWS = 4096
INNER = 1024
COLUMNS = 4096


def draw_left_values(key, part):
    first_key, second_key = jax.random.split(key)
    position = jnp.arange(ROWS, dtype=jnp.float32) / ROWS
    ramp_factor = jnp.power(3.0, 0.5 * position)[:, None]
    base_values = jax.random.uniform(first_key, (ROWS, INNER), jnp.float32, 0.1, 1.0)
    row_scale = jnp.exp(jax.random.uniform(second_key, (ROWS, 1), jnp.float32, 0.0, 0.5 * math.log(10.0)))
    return (base_values * ramp_factor * row_scale).astype(jnp.bfloat16)


def draw_left_pattern(key, part):
    count_key, row_key, group_key, score_key = jax.random.split(key, 4)
    groups = BLOCK_INNER // LEFT_GROUP
    counts = jax.random.randint(count_key, (BLOCK_ROWS, groups), 1, LEFT_SLOTS + 1)
    full_row = jax.random.randint(row_key, (), 0, BLOCK_ROWS)
    full_group = jax.random.randint(group_key, (), 0, groups)
    chosen = (jnp.arange(BLOCK_ROWS)[:, None] == full_row) & (jnp.arange(groups)[None, :] == full_group)
    counts = jnp.where(chosen, LEFT_SLOTS, counts)
    columns = jnp.arange(BLOCK_INNER)
    forced = columns[None, :] == (jnp.arange(BLOCK_ROWS) % BLOCK_INNER)[:, None]
    raw_scores = jax.random.randint(score_key, (BLOCK_ROWS, BLOCK_INNER), 0, 65536)
    scores = raw_scores * BLOCK_INNER + columns[None, :] + forced.astype(jnp.int32) * 33554432
    grouped = scores.reshape(BLOCK_ROWS, groups, LEFT_GROUP)
    ranking = jnp.sum((grouped[:, :, None, :] > grouped[:, :, :, None]).astype(jnp.int32), axis=3)
    chosen_mask = ranking < counts[:, :, None]
    return chosen_mask.reshape(BLOCK_ROWS, BLOCK_INNER).astype(jnp.int32)


def draw_right_pattern(key, part):
    count_key, row_key, group_key, score_key = jax.random.split(key, 4)
    groups = BLOCK_COLS // COL_BLOCKS
    counts = jax.random.randint(count_key, (BLOCK_INNER, groups), 1, SLOTS + 1)
    full_row = jax.random.randint(row_key, (), 0, BLOCK_INNER)
    full_group = jax.random.randint(group_key, (), 0, groups)
    chosen = (jnp.arange(BLOCK_INNER)[:, None] == full_row) & (jnp.arange(groups)[None, :] == full_group)
    counts = jnp.where(chosen, SLOTS, counts)
    columns = jnp.arange(BLOCK_COLS)
    forced = columns[None, :] % BLOCK_INNER == jnp.arange(BLOCK_INNER)[:, None]
    raw_scores = jax.random.randint(score_key, (BLOCK_INNER, BLOCK_COLS), 0, 65536)
    scores = raw_scores * BLOCK_COLS + columns[None, :] + forced.astype(jnp.int32) * 33554432
    grouped = scores.reshape(BLOCK_INNER, groups, COL_BLOCKS)
    ranking = jnp.sum((grouped[:, :, None, :] > grouped[:, :, :, None]).astype(jnp.int32), axis=3)
    chosen_mask = ranking < counts[:, :, None]
    return chosen_mask.reshape(BLOCK_INNER, BLOCK_COLS).astype(jnp.int32)


def block_levels(rng, extent, cuts, smallest, top_value):
    def one(dim, blocks):
        heights = jax.random.uniform(jax.random.fold_in(jax.random.fold_in(rng, 6), dim), (blocks,), jnp.float32, smallest / len(cuts), top_value / len(cuts))
        return jnp.repeat(jnp.exp(heights), extent[dim] // blocks).reshape((-1,) + (1,) * (len(extent) - dim - 1))

    level = one(*cuts[0])
    for cut in cuts[1:]:
        level = level * one(*cut)
    return level


def setup_inputs(seed: int = 0) -> dict:
    keys = jax.random.split(jax.random.key(seed), 5)
    left_values = draw_left_values(jax.random.fold_in(keys[4], 71), 0)
    left_pattern = draw_left_pattern(jax.random.fold_in(keys[4], 71), 0)
    right_values = jnp.clip(0.099609375 + 0.9003906 * jax.random.uniform(keys[2], (INNER, COLUMNS), jnp.float32) ** block_levels(keys[2], (INNER, COLUMNS), ((0, 8), (1, 4)), -0.2, 0.2), 0.099609375, 1.0).astype(jnp.bfloat16)
    right_pattern = draw_right_pattern(jax.random.fold_in(keys[4], 71), 0)
    return dict(left_values=left_values, left_pattern=left_pattern, right_values=right_values, right_pattern=right_pattern)


def expand(values, pattern):
    block_rows, block_cols = pattern.shape
    height, width = values.shape
    shaped = values.reshape(block_rows, height // block_rows, block_cols, width // block_cols)
    masked = shaped * pattern.astype(values.dtype)[:, None, :, None]
    return masked.reshape(height, width)


def reference(left_values, left_pattern, right_values, right_pattern):
    left = expand(left_values, left_pattern).astype(jnp.float32)
    right = expand(right_values, right_pattern).astype(jnp.float32)
    product = jnp.dot(left, right, preferred_element_type=jnp.float32)
    inflated = product * product
    column_mean = jnp.sum(inflated, axis=0) / ROWS
    return inflated / column_mean[None, :]
```

```python
import functools

import jax
import jax.numpy as jnp
from jax import lax
from jax.experimental import pallas as pl
from jax.experimental.pallas import tpu as pltpu
from jax.sharding import PartitionSpec as P

BLOCK = 128
MESH = pl.DeviceIdType.MESH


class Gather:
    def __init__(self, axis, outer, inner, held, send_sem, recv_sem):
        self.axis, self.outer, self.inner = axis, outer, inner
        self.held, self.send_sem, self.recv_sem = held, send_sem, recv_sem
        me = lax.axis_index(axis)
        self.me, self.o, self.i = me, me // inner, me % inner

    def copy(self, slot, lane, target):
        return pltpu.make_async_remote_copy(
            src_ref=self.held.at[slot],
            dst_ref=self.held.at[slot],
            send_sem=self.send_sem.at[lane, slot],
            recv_sem=self.recv_sem.at[slot],
            device_id={self.axis: target},
            device_id_type=MESH,
        )

    def each_outer(self, slot, step, act):
        target = self.o + step

        @pl.when((target >= 0) & (target < self.outer))
        def _():
            act(self.copy(slot, 0 if step == 1 else 1, target * self.inner + self.i))

    def each_inner(self, slot, step, act):
        target = self.i + step

        @pl.when((target >= 0) & (target < self.inner))
        def _():
            act(self.copy(slot, 2 if step == 1 else 3, self.o * self.inner + target))

    def visit_own(self, act):
        for step in (1, -1):
            self.each_outer(self.me, step, act)
        for step in (1, -1):
            self.each_inner(self.me, step, act)

    def visit_outer(self, o, wait, act):
        slot = o * self.inner + self.i
        if wait:
            self.copy(slot, 0, self.me).wait_recv()

        @pl.when(o < self.o)
        def _():
            self.each_outer(slot, 1, act)

        @pl.when(o > self.o)
        def _():
            self.each_outer(slot, -1, act)

        for step in (1, -1):
            self.each_inner(slot, step, act)

    def visit_inner(self, o, wait, act):
        for distance in range(1, self.inner):
            for step in (1, -1):
                i = self.i + step * distance

                @pl.when((i >= 0) & (i < self.inner))
                def _():
                    slot = o * self.inner + i
                    if wait:
                        self.copy(slot, 0, self.me).wait_recv()
                    self.each_inner(slot, -step, act)

    def place(self, q):
        distance = (q + 1) // 2
        sign = 2 * (q % 2) - 1
        o = self.o + sign * distance
        return o, (o >= 0) & (o < self.outer)


def start(copy):
    copy.start()


def wait_send(copy):
    copy.wait_send()


def kernel(
    sizes,
    left_pattern, right_pattern, left_values, right_values,
    product, scale,
    left_in, right_in, left_held, right_held, left_dense, sums,
    in_sem, left_send, left_recv, right_send, right_recv, sum_send, sum_recv,
):
    row_count, col_count, y_size, x_size = sizes
    rows_local, inner_local = left_in.shape
    left_blocks = rows_local // BLOCK
    group = inner_local // BLOCK
    left_slots = left_held.shape[2]
    col_blocks = right_in.shape[1] // BLOCK
    slots = right_held.shape[1]
    z_size = col_count // x_size
    row, col = lax.axis_index("row"), lax.axis_index("col")

    barrier = pltpu.get_barrier_semaphore()

    @pl.loop(1, col_count)
    def _(d):
        pl.semaphore_signal(
            barrier, inc=1, device_id={"col": (col + d) % col_count}, device_id_type=MESH
        )

    @pl.loop(1, row_count)
    def _(d):
        pl.semaphore_signal(
            barrier, inc=1, device_id={"row": (row + d) % row_count}, device_id_type=MESH
        )

    right_load = pltpu.make_async_copy(right_values, right_in, in_sem.at[0])
    left_load = pltpu.make_async_copy(left_values, left_in, in_sem.at[1])
    right_load.start()
    left_load.start()

    def pick(ones, wanted, candidate):
        before, found = 0, [None] * wanted
        for k, one in enumerate(ones):
            block = candidate(k)
            for s in range(min(k + 1, wanted)):
                if k == s:
                    found[s] = block
                else:
                    found[s] = jnp.where((one != 0) & (before == s), block, found[s])
            before = before + one
        return found

    def unpick(one, before, packed):
        block = jnp.zeros_like(packed[0])
        for s, value in enumerate(packed):
            block = jnp.where((one != 0) & (before == s), value, block)
        return block

    right = Gather("col", z_size, x_size, right_held, right_send, right_recv)
    left = Gather("row", y_size, row_count // y_size, left_held, left_send, left_recv)

    ones = [right_pattern[col, row * col_blocks + j] for j in range(col_blocks)]
    right_load.wait()
    picks = pick(ones, slots, lambda j: right_in[:, j * BLOCK:(j + 1) * BLOCK])
    for s in range(slots):
        right_held[col, s] = picks[s]
    pl.semaphore_wait(barrier, col_count - 1 + row_count - 1)
    right.visit_own(start)

    left_load.wait()
    for b in range(left_blocks):
        ones = [left_pattern[col * left_blocks + b, row * group + k] for k in range(group)]
        at = slice(b * BLOCK, (b + 1) * BLOCK)
        picks = pick(ones, left_slots, lambda k: left_in[at, k * BLOCK:(k + 1) * BLOCK])
        for s in range(left_slots):
            left_held[row, b, s] = picks[s]
    left.visit_own(start)

    product[...] = jnp.zeros_like(product)

    @pl.loop(1, 2 * y_size - 1)
    def _(q):
        o, valid = left.place(q)

        @pl.when(valid)
        def _():
            left.visit_outer(o, True, start)

    @pl.loop(0, y_size)
    def _(o):
        left.visit_inner(o, True, start)

    @pl.loop(0, row_count * group)
    def _(k):
        g, within = k // group, k % group
        at = pl.ds(pl.multiple_of((k % x_size) * BLOCK, BLOCK), BLOCK)
        for b in range(left_blocks):
            block_row = col * left_blocks + b
            here = left_pattern[block_row, k]
            before = 0
            for m in range(group - 1):
                before = before + jnp.where(m < within, left_pattern[block_row, g * group + m], 0)
            left_dense[k // x_size, b * BLOCK:(b + 1) * BLOCK, at] = unpick(
                here, before, [left_held[g, b, s] for s in range(left_slots)]
            )

    def multiply(o):
        right.visit_inner(o, True, start)
        ones, ranks = [], []
        for i in range(x_size):
            k = o * x_size + i
            line = [right_pattern[k, row * col_blocks + j] for j in range(col_blocks)]
            rank = [0] * col_blocks
            for j in range(1, col_blocks):
                rank[j] = rank[j - 1] + line[j - 1]
            ones.append(line)
            ranks.append(rank)

        def dense(i, j):
            packed = [right_held[o * x_size + i, s] for s in range(slots)]
            return unpick(ones[i][j], ranks[i][j], packed)

        for j in range(0, col_blocks, 2):
            block = jnp.concatenate(
                [jnp.concatenate([dense(i, j), dense(i, j + 1)], axis=1) for i in range(x_size)],
                axis=0,
            )
            at = pl.ds(j * BLOCK, 2 * BLOCK)
            product[:, at] += jnp.dot(left_dense[o], block, preferred_element_type=jnp.float32)

    @pl.loop(0, 2 * z_size - 1 + 2)
    def _(q):
        o, valid = right.place(q)

        @pl.when((q > 0) & valid)
        def _():
            right.visit_outer(o, True, start)

        late, late_valid = right.place(jnp.maximum(q - 2, 0))

        @pl.when((q >= 2) & late_valid)
        def _():
            multiply(late)

    for j in range(col_blocks):
        part = product[:, j * BLOCK:(j + 1) * BLOCK]
        sums[col, j:j + 1, :] = jnp.sum(part * part, axis=0, keepdims=True)

    def sum_copy(d):
        return pltpu.make_async_remote_copy(
            src_ref=sums.at[col],
            dst_ref=sums.at[col],
            send_sem=sum_send.at[d],
            recv_sem=sum_recv.at[col],
            device_id={"col": (col + d) % col_count},
            device_id_type=MESH,
        )

    @pl.loop(1, col_count)
    def _(d):
        sum_copy(d).start()

    right.visit_own(wait_send)
    left.visit_own(wait_send)

    @pl.loop(1, 2 * y_size - 1)
    def _(q):
        o, valid = left.place(q)

        @pl.when(valid)
        def _():
            left.visit_outer(o, False, wait_send)

    @pl.loop(0, y_size)
    def _(o):
        left.visit_inner(o, False, wait_send)

    @pl.loop(1, 2 * z_size - 1)
    def _(q):
        o, valid = right.place(q)

        @pl.when(valid)
        def _():
            right.visit_outer(o, False, wait_send)

    @pl.loop(0, z_size)
    def _(o):
        right.visit_inner(o, False, wait_send)

    @pl.loop(1, col_count)
    def _(d):
        sum_copy(d).wait_send()
        source = (col + d) % col_count
        pltpu.make_async_remote_copy(
            src_ref=sums.at[source],
            dst_ref=sums.at[source],
            send_sem=sum_send.at[d],
            recv_sem=sum_recv.at[source],
            device_id={"col": source},
            device_id_type=MESH,
        ).wait_recv()

    total = sums[0]
    for c in range(1, col_count):
        total = total + sums[c]
    factor = (rows_local * col_count) / total
    for j in range(col_blocks):
        scale[0:1, j * BLOCK:(j + 1) * BLOCK] = factor[j:j + 1, :]


def shards(row_count, col_count, left_values, left_pattern, right_values, right_pattern):
    rows_local, inner_local = left_values.shape
    inner_rows, cols_local = right_values.shape
    y_size = row_count // 2
    x_size = y_size if col_count % y_size == 0 else 1
    group = inner_local // BLOCK
    left_slots = max(1, group // 2)
    left_blocks = rows_local // BLOCK
    col_blocks = cols_local // BLOCK
    slots = col_blocks // 2
    inner = row_count * inner_local
    dma = pltpu.SemaphoreType.DMA
    product, scale = pl.pallas_call(
        functools.partial(kernel, (row_count, col_count, y_size, x_size)),
        out_shape=(
            jax.ShapeDtypeStruct((rows_local, cols_local), jnp.float32),
            jax.ShapeDtypeStruct((1, cols_local), jnp.float32),
        ),
        in_specs=[pl.BlockSpec(memory_space=pltpu.SMEM)] * 2 + [pl.BlockSpec(memory_space=pl.ANY)] * 2,
        out_specs=(pl.BlockSpec(memory_space=pltpu.VMEM),) * 2,
        scratch_shapes=[
            pltpu.VMEM((rows_local, inner_local), jnp.bfloat16),
            pltpu.VMEM((inner_rows, cols_local), jnp.bfloat16),
            pltpu.VMEM((row_count, left_blocks, left_slots, BLOCK, BLOCK), jnp.bfloat16),
            pltpu.VMEM((col_count, slots, BLOCK, BLOCK), jnp.bfloat16),
            pltpu.VMEM((inner // (x_size * BLOCK), rows_local, x_size * BLOCK), jnp.bfloat16),
            pltpu.VMEM((col_count, col_blocks, BLOCK), jnp.float32),
            dma((2,)),
            dma((4, row_count)),
            dma((row_count,)),
            dma((4, col_count)),
            dma((col_count,)),
            dma((col_count,)),
            dma((col_count,)),
        ],
        compiler_params=pltpu.CompilerParams(
            collective_id=0, has_side_effects=True, vmem_limit_bytes=32 * 1024 * 1024
        ),
    )(left_pattern, right_pattern, left_values, right_values)
    return product * product * scale


def solution(mesh):
    return jax.shard_map(
        functools.partial(shards, mesh.shape["row"], mesh.shape["col"]),
        mesh=mesh,
        in_specs=(P("col", "row"), P(), P("col", "row"), P()),
        out_specs=P("col", "row"),
        check_vma=False,
    )
```

```python
import functools

import jax
import jax.numpy as jnp
from jax import lax
from jax.experimental import pallas as pl
from jax.experimental.pallas import tpu as pltpu
from jax.sharding import PartitionSpec as P

BLOCK = 128
MESH = pl.DeviceIdType.MESH


class Gather:
    def __init__(self, axis, outer, inner, held, send_sem, recv_sem):
        self.axis, self.outer, self.inner = axis, outer, inner
        self.held, self.send_sem, self.recv_sem = held, send_sem, recv_sem
        self.parts = recv_sem.shape[1]
        self.depth = held.shape[1] // self.parts
        me = lax.axis_index(axis)
        self.me, self.o, self.i = me, me // inner, me % inner

    def copy(self, slot, part, lane, target):
        piece = self.held.at[slot, pl.ds(part * self.depth, self.depth)]
        return pltpu.make_async_remote_copy(
            src_ref=piece,
            dst_ref=piece,
            send_sem=self.send_sem.at[lane, slot, part],
            recv_sem=self.recv_sem.at[slot, part],
            device_id={self.axis: target},
            device_id_type=MESH,
        )

    def each_outer(self, slot, part, step, act):
        target = self.o + step

        @pl.when((target >= 0) & (target < self.outer))
        def _():
            act(self.copy(slot, part, 0 if step == 1 else 1, target * self.inner + self.i))

    def each_inner(self, slot, part, step, act):
        target = self.i + step

        @pl.when((target >= 0) & (target < self.inner))
        def _():
            act(self.copy(slot, part, 2 if step == 1 else 3, self.o * self.inner + target))

    def visit_own(self, act):
        for part in range(self.parts):
            for step in (1, -1):
                self.each_outer(self.me, part, step, act)
            for step in (1, -1):
                self.each_inner(self.me, part, step, act)

    def visit_outer(self, o, wait, act):
        slot = o * self.inner + self.i
        for part in range(self.parts):
            if wait:
                self.copy(slot, part, 0, self.me).wait_recv()

            @pl.when(o < self.o)
            def _():
                self.each_outer(slot, part, 1, act)

            @pl.when(o > self.o)
            def _():
                self.each_outer(slot, part, -1, act)

            for step in (1, -1):
                self.each_inner(slot, part, step, act)

    def visit_inner(self, o, wait, act):
        for distance in range(1, self.inner):
            for step in (1, -1):
                i = self.i + step * distance

                @pl.when((i >= 0) & (i < self.inner))
                def _():
                    slot = o * self.inner + i
                    for part in range(self.parts):
                        if wait:
                            self.copy(slot, part, 0, self.me).wait_recv()
                        self.each_inner(slot, part, -step, act)

    def place(self, q):
        distance = (q + 1) // 2
        sign = 2 * (q % 2) - 1
        o = self.o + sign * distance
        return o, (o >= 0) & (o < self.outer)


def start(copy):
    copy.start()


def wait_send(copy):
    copy.wait_send()


def kernel(
    sizes,
    left_ones, right_ones, left_values, right_values,
    product, scale,
    left_pattern, right_pattern, left_in, right_in, left_held, right_held, left_dense, sums,
    in_sem, left_send, left_recv, right_send, right_recv, sum_send, sum_recv,
):
    row_count, col_count, y_size, x_size = sizes
    rows_local, inner_local = left_in.shape
    left_blocks = rows_local // BLOCK
    group = inner_local // BLOCK
    left_slots = left_held.shape[2]
    col_blocks = right_in.shape[1] // BLOCK
    slots = right_held.shape[1]
    z_size = col_count // x_size
    row, col = lax.axis_index("row"), lax.axis_index("col")

    barrier = pltpu.get_barrier_semaphore()

    @pl.loop(1, col_count)
    def _(d):
        pl.semaphore_signal(
            barrier, inc=1, device_id={"col": (col + d) % col_count}, device_id_type=MESH
        )

    @pl.loop(1, row_count)
    def _(d):
        pl.semaphore_signal(
            barrier, inc=1, device_id={"row": (row + d) % row_count}, device_id_type=MESH
        )

    right_load = pltpu.make_async_copy(right_values, right_in, in_sem.at[0])
    left_load = pltpu.make_async_copy(left_values, left_in, in_sem.at[1])
    left_ones_load = pltpu.make_async_copy(left_ones, left_pattern, in_sem.at[2])
    right_ones_load = pltpu.make_async_copy(right_ones, right_pattern, in_sem.at[3])
    right_ones_load.start()
    right_load.start()
    left_ones_load.start()
    left_load.start()

    def pick(ones, wanted, candidate):
        before, found = 0, [None] * wanted
        for k, one in enumerate(ones):
            block = candidate(k)
            for s in range(min(k + 1, wanted)):
                if k == s:
                    found[s] = block
                else:
                    found[s] = jnp.where((one != 0) & (before == s), block, found[s])
            before = before + one
        return found

    def unpick(one, before, packed):
        block = jnp.zeros_like(packed[0])
        for s, value in enumerate(packed):
            block = jnp.where((one != 0) & (before == s), value, block)
        return block

    right = Gather("col", z_size, x_size, right_held, right_send, right_recv)
    left = Gather("row", y_size, row_count // y_size, left_held, left_send, left_recv)

    right_ones_load.wait()
    ones = [right_pattern[col, row * col_blocks + j] for j in range(col_blocks)]
    right_load.wait()
    picks = pick(ones, slots, lambda j: right_in[:, j * BLOCK:(j + 1) * BLOCK])
    for s in range(slots):
        right_held[col, s] = picks[s]
    pl.semaphore_wait(barrier, col_count - 1 + row_count - 1)
    right.visit_own(start)

    left_ones_load.wait()
    left_load.wait()
    for b in range(left_blocks):
        ones = [left_pattern[row * group + k, col * left_blocks + b] for k in range(group)]
        at = slice(b * BLOCK, (b + 1) * BLOCK)
        picks = pick(ones, left_slots, lambda k: left_in[at, k * BLOCK:(k + 1) * BLOCK])
        for s in range(left_slots):
            left_held[row, b, s] = picks[s]
    left.visit_own(start)

    product[...] = jnp.zeros_like(product)

    @pl.loop(1, 2 * y_size - 1)
    def _(q):
        o, valid = left.place(q)

        @pl.when(valid)
        def _():
            left.visit_outer(o, True, start)

    @pl.loop(0, y_size)
    def _(o):
        left.visit_inner(o, True, start)

    @pl.loop(0, row_count * group)
    def _(k):
        g, within = k // group, k % group
        at = pl.ds(pl.multiple_of((k % x_size) * BLOCK, BLOCK), BLOCK)
        for b in range(left_blocks):
            block_row = col * left_blocks + b
            here = left_pattern[k, block_row]
            before = 0
            for m in range(group - 1):
                before = before + jnp.where(m < within, left_pattern[g * group + m, block_row], 0)
            left_dense[k // x_size, b * BLOCK:(b + 1) * BLOCK, at] = unpick(
                here, before, [left_held[g, b, s] for s in range(left_slots)]
            )

    def multiply(o):
        right.visit_inner(o, True, start)
        ones, ranks = [], []
        for i in range(x_size):
            k = o * x_size + i
            line = [right_pattern[k, row * col_blocks + j] for j in range(col_blocks)]
            rank = [0] * col_blocks
            for j in range(1, col_blocks):
                rank[j] = rank[j - 1] + line[j - 1]
            ones.append(line)
            ranks.append(rank)

        def dense(i, j):
            packed = [right_held[o * x_size + i, s] for s in range(slots)]
            return unpick(ones[i][j], ranks[i][j], packed)

        for j in range(0, col_blocks, 2):
            block = jnp.concatenate(
                [jnp.concatenate([dense(i, j), dense(i, j + 1)], axis=1) for i in range(x_size)],
                axis=0,
            )
            at = pl.ds(j * BLOCK, 2 * BLOCK)
            product[:, at] += jnp.dot(left_dense[o], block, preferred_element_type=jnp.float32)

    @pl.loop(0, 2 * z_size - 1 + 2)
    def _(q):
        o, valid = right.place(q)

        @pl.when((q > 0) & valid)
        def _():
            right.visit_outer(o, True, start)

        late, late_valid = right.place(jnp.maximum(q - 2, 0))

        @pl.when((q >= 2) & late_valid)
        def _():
            multiply(late)

    for j in range(col_blocks):
        part = product[:, j * BLOCK:(j + 1) * BLOCK]
        sums[col, j:j + 1, :] = jnp.sum(part * part, axis=0, keepdims=True)

    def sum_copy(d):
        return pltpu.make_async_remote_copy(
            src_ref=sums.at[col],
            dst_ref=sums.at[col],
            send_sem=sum_send.at[d],
            recv_sem=sum_recv.at[col],
            device_id={"col": (col + d) % col_count},
            device_id_type=MESH,
        )

    @pl.loop(1, col_count)
    def _(d):
        sum_copy(d).start()

    right.visit_own(wait_send)
    left.visit_own(wait_send)

    @pl.loop(1, 2 * y_size - 1)
    def _(q):
        o, valid = left.place(q)

        @pl.when(valid)
        def _():
            left.visit_outer(o, False, wait_send)

    @pl.loop(0, y_size)
    def _(o):
        left.visit_inner(o, False, wait_send)

    @pl.loop(1, 2 * z_size - 1)
    def _(q):
        o, valid = right.place(q)

        @pl.when(valid)
        def _():
            right.visit_outer(o, False, wait_send)

    @pl.loop(0, z_size)
    def _(o):
        right.visit_inner(o, False, wait_send)

    @pl.loop(1, col_count)
    def _(d):
        sum_copy(d).wait_send()
        source = (col + d) % col_count
        pltpu.make_async_remote_copy(
            src_ref=sums.at[source],
            dst_ref=sums.at[source],
            send_sem=sum_send.at[d],
            recv_sem=sum_recv.at[source],
            device_id={"col": source},
            device_id_type=MESH,
        ).wait_recv()

    total = sums[0]
    for c in range(1, col_count):
        total = total + sums[c]
    factor = (rows_local * col_count) / total
    for j in range(col_blocks):
        scale[0:1, j * BLOCK:(j + 1) * BLOCK] = factor[j:j + 1, :]


def shards(row_count, col_count, left_values, left_pattern, right_values, right_pattern):
    rows_local, inner_local = left_values.shape
    inner_rows, cols_local = right_values.shape
    y_size = row_count // 2
    x_size = y_size if col_count % y_size == 0 else 1
    group = inner_local // BLOCK
    left_slots = max(1, group // 2)
    left_blocks = rows_local // BLOCK
    col_blocks = cols_local // BLOCK
    slots = col_blocks // 2
    parts = 2
    inner = row_count * inner_local
    dma = pltpu.SemaphoreType.DMA
    operands = (left_pattern.T, right_pattern, left_values, right_values)
    product, scale = pl.pallas_call(
        functools.partial(kernel, (row_count, col_count, y_size, x_size)),
        out_shape=(
            jax.ShapeDtypeStruct((rows_local, cols_local), jnp.float32),
            jax.ShapeDtypeStruct((1, cols_local), jnp.float32),
        ),
        in_specs=[pl.BlockSpec(memory_space=pltpu.HBM)] * 4,
        out_specs=(pl.BlockSpec(memory_space=pltpu.VMEM),) * 2,
        scratch_shapes=[
            pltpu.SMEM(left_pattern.shape[::-1], jnp.int32),
            pltpu.SMEM(right_pattern.shape, jnp.int32),
            pltpu.VMEM((rows_local, inner_local), jnp.bfloat16),
            pltpu.VMEM((inner_rows, cols_local), jnp.bfloat16),
            pltpu.VMEM((row_count, left_blocks, left_slots, BLOCK, BLOCK), jnp.bfloat16),
            pltpu.VMEM((col_count, slots, BLOCK, BLOCK), jnp.bfloat16),
            pltpu.VMEM((inner // (x_size * BLOCK), rows_local, x_size * BLOCK), jnp.bfloat16),
            pltpu.VMEM((col_count, col_blocks, BLOCK), jnp.float32),
            dma((4,)),
            dma((4, row_count, 1)),
            dma((row_count, 1)),
            dma((4, col_count, parts)),
            dma((col_count, parts)),
            dma((col_count,)),
            dma((col_count,)),
        ],
        compiler_params=pltpu.CompilerParams(
            collective_id=0, has_side_effects=True, vmem_limit_bytes=32 * 1024 * 1024
        ),
    )(*(pltpu.with_memory_space_constraint(x, pltpu.HBM) for x in operands))
    return product * product * scale


def solution(mesh):
    return jax.shard_map(
        functools.partial(shards, mesh.shape["row"], mesh.shape["col"]),
        mesh=mesh,
        in_specs=(P("col", "row"), P(), P("col", "row"), P()),
        out_specs=P("col", "row"),
        check_vma=False,
    )
```

```python
import functools

import jax
import jax.numpy as jnp
from jax import lax
from jax.experimental import pallas as pl
from jax.experimental.pallas import tpu as pltpu
from jax.sharding import PartitionSpec as P

BLOCK = 128
MESH = pl.DeviceIdType.MESH


class Gather:
    def __init__(self, axis, outer, inner, held, send_sem, recv_sem):
        self.axis, self.outer, self.inner = axis, outer, inner
        self.held, self.send_sem, self.recv_sem = held, send_sem, recv_sem
        self.parts = recv_sem.shape[1]
        self.depth = held.shape[1] // self.parts
        me = lax.axis_index(axis)
        self.me, self.o, self.i = me, me // inner, me % inner

    def copy(self, slot, part, lane, target):
        piece = self.held.at[slot, pl.ds(part * self.depth, self.depth)]
        return pltpu.make_async_remote_copy(
            src_ref=piece,
            dst_ref=piece,
            send_sem=self.send_sem.at[lane, slot, part],
            recv_sem=self.recv_sem.at[slot, part],
            device_id={self.axis: target},
            device_id_type=MESH,
        )

    def each_outer(self, slot, part, step, act):
        target = self.o + step

        @pl.when((target >= 0) & (target < self.outer))
        def _():
            act(self.copy(slot, part, 0 if step == 1 else 1, target * self.inner + self.i))

    def each_inner(self, slot, part, step, act):
        target = self.i + step

        @pl.when((target >= 0) & (target < self.inner))
        def _():
            act(self.copy(slot, part, 2 if step == 1 else 3, self.o * self.inner + target))

    def visit_own(self, act):
        for part in range(self.parts):
            for step in (1, -1):
                self.each_outer(self.me, part, step, act)
            for step in (1, -1):
                self.each_inner(self.me, part, step, act)

    def visit_outer(self, o, wait, act):
        slot = o * self.inner + self.i
        for part in range(self.parts):
            if wait:
                self.copy(slot, part, 0, self.me).wait_recv()

            @pl.when(o < self.o)
            def _():
                self.each_outer(slot, part, 1, act)

            @pl.when(o > self.o)
            def _():
                self.each_outer(slot, part, -1, act)

            for step in (1, -1):
                self.each_inner(slot, part, step, act)

    def visit_inner(self, o, wait, act):
        for distance in range(1, self.inner):
            for step in (1, -1):
                i = self.i + step * distance

                @pl.when((i >= 0) & (i < self.inner))
                def _():
                    slot = o * self.inner + i
                    for part in range(self.parts):
                        if wait:
                            self.copy(slot, part, 0, self.me).wait_recv()
                        self.each_inner(slot, part, -step, act)

    def place(self, q):
        o = jnp.where(q < self.outer, self.o - q, self.o + q - self.outer + 1)
        return o, (o >= 0) & (o < self.outer)

    def greet(self, barrier):
        count = 0
        for step in (1, -1):
            for own, size, stride in ((self.o, self.outer, self.inner), (self.i, self.inner, 1)):
                there = (own + step >= 0) & (own + step < size)

                @pl.when(there)
                def _():
                    pl.semaphore_signal(
                        barrier, inc=1, device_id={self.axis: self.me + step * stride}, device_id_type=MESH
                    )

                count = count + jnp.where(there, 1, 0)
        return count


def start(copy):
    copy.start()


def wait_send(copy):
    copy.wait_send()


def kernel(
    sizes,
    left_ones, right_ones, left_values, right_values,
    product, scale,
    left_pattern, right_pattern, left_in, right_in, left_held, right_held, left_dense, sums,
    in_sem, left_send, left_recv, right_send, right_recv, sum_send, sum_recv,
):
    row_count, col_count, y_size, x_size = sizes
    rows_local, inner_local = left_in.shape
    left_blocks = rows_local // BLOCK
    group = inner_local // BLOCK
    left_slots = left_held.shape[2]
    col_blocks = right_in.shape[1] // BLOCK
    slots = right_held.shape[1]
    z_size = col_count // x_size
    row, col = lax.axis_index("row"), lax.axis_index("col")

    barrier = pltpu.get_barrier_semaphore()

    right = Gather("col", z_size, x_size, right_held, right_send, right_recv)
    left = Gather("row", y_size, row_count // y_size, left_held, left_send, left_recv)
    neighbours = right.greet(barrier) + left.greet(barrier)

    right_load = pltpu.make_async_copy(right_values, right_in, in_sem.at[0])
    left_load = pltpu.make_async_copy(left_values, left_in, in_sem.at[1])
    left_ones_load = pltpu.make_async_copy(left_ones, left_pattern, in_sem.at[2])
    right_ones_load = pltpu.make_async_copy(right_ones, right_pattern, in_sem.at[3])
    right_ones_load.start()
    right_load.start()
    left_ones_load.start()
    left_load.start()

    def pick(ones, wanted, candidate):
        before, found = 0, [None] * wanted
        for k, one in enumerate(ones):
            block = candidate(k)
            for s in range(min(k + 1, wanted)):
                if k == s:
                    found[s] = block
                else:
                    found[s] = jnp.where((one != 0) & (before == s), block, found[s])
            before = before + one
        return found

    def unpick(one, before, packed):
        block = jnp.zeros_like(packed[0])
        for s, value in enumerate(packed):
            block = jnp.where((one != 0) & (before == s), value, block)
        return block

    right_ones_load.wait()
    ones = [right_pattern[col, row * col_blocks + j] for j in range(col_blocks)]
    right_load.wait()
    picks = pick(ones, slots, lambda j: right_in[:, j * BLOCK:(j + 1) * BLOCK])
    for s in range(slots):
        right_held[col, s] = picks[s]
    pl.semaphore_wait(barrier, neighbours)
    right.visit_own(start)

    left_ones_load.wait()
    left_load.wait()
    for b in range(left_blocks):
        ones = [left_pattern[row * group + k, col * left_blocks + b] for k in range(group)]
        at = slice(b * BLOCK, (b + 1) * BLOCK)
        picks = pick(ones, left_slots, lambda k: left_in[at, k * BLOCK:(k + 1) * BLOCK])
        for s in range(left_slots):
            left_held[row, b, s] = picks[s]
    left.visit_own(start)

    product[...] = jnp.zeros_like(product)

    def finish_left():
        @pl.loop(1, 2 * y_size - 1)
        def _(q):
            o, valid = left.place(q)

            @pl.when(valid)
            def _():
                left.visit_outer(o, True, start)

        @pl.loop(0, y_size)
        def _(o):
            left.visit_inner(o, True, start)

        @pl.loop(0, row_count * group)
        def _(k):
            g, within = k // group, k % group
            at = pl.ds(pl.multiple_of((k % x_size) * BLOCK, BLOCK), BLOCK)
            for b in range(left_blocks):
                block_row = col * left_blocks + b
                here = left_pattern[k, block_row]
                before = 0
                for m in range(group - 1):
                    before = before + jnp.where(m < within, left_pattern[g * group + m, block_row], 0)
                left_dense[k // x_size, b * BLOCK:(b + 1) * BLOCK, at] = unpick(
                    here, before, [left_held[g, b, s] for s in range(left_slots)]
                )

    def multiply(o):
        right.visit_inner(o, True, start)
        ones, ranks = [], []
        for i in range(x_size):
            k = o * x_size + i
            line = [right_pattern[k, row * col_blocks + j] for j in range(col_blocks)]
            rank = [0] * col_blocks
            for j in range(1, col_blocks):
                rank[j] = rank[j - 1] + line[j - 1]
            ones.append(line)
            ranks.append(rank)

        def dense(i, j):
            packed = [right_held[o * x_size + i, s] for s in range(slots)]
            return unpick(ones[i][j], ranks[i][j], packed)

        for j in range(0, col_blocks, 2):
            block = jnp.concatenate(
                [jnp.concatenate([dense(i, j), dense(i, j + 1)], axis=1) for i in range(x_size)],
                axis=0,
            )
            at = pl.ds(j * BLOCK, 2 * BLOCK)
            product[:, at] += jnp.dot(left_dense[o], block, preferred_element_type=jnp.float32)

    @pl.loop(0, 2 * z_size)
    def _(q):
        o, valid = right.place(q)

        @pl.when((q > 0) & (q < 2 * z_size - 1) & valid)
        def _():
            right.visit_outer(o, True, start)

        @pl.when(q == 1)
        def _():
            finish_left()

        late, late_valid = right.place(jnp.maximum(q - 1, 0))

        @pl.when((q >= 1) & late_valid)
        def _():
            multiply(late)

    for j in range(col_blocks):
        part = product[:, j * BLOCK:(j + 1) * BLOCK]
        sums[col, j:j + 1, :] = jnp.sum(part * part, axis=0, keepdims=True)

    def sum_copy(d):
        return pltpu.make_async_remote_copy(
            src_ref=sums.at[col],
            dst_ref=sums.at[col],
            send_sem=sum_send.at[d],
            recv_sem=sum_recv.at[col],
            device_id={"col": (col + d) % col_count},
            device_id_type=MESH,
        )

    @pl.loop(1, col_count)
    def _(d):
        sum_copy(d).start()

    right.visit_own(wait_send)
    left.visit_own(wait_send)

    @pl.loop(1, 2 * y_size - 1)
    def _(q):
        o, valid = left.place(q)

        @pl.when(valid)
        def _():
            left.visit_outer(o, False, wait_send)

    @pl.loop(0, y_size)
    def _(o):
        left.visit_inner(o, False, wait_send)

    @pl.loop(1, 2 * z_size - 1)
    def _(q):
        o, valid = right.place(q)

        @pl.when(valid)
        def _():
            right.visit_outer(o, False, wait_send)

    @pl.loop(0, z_size)
    def _(o):
        right.visit_inner(o, False, wait_send)

    @pl.loop(1, col_count)
    def _(d):
        sum_copy(d).wait_send()
        source = (col + d) % col_count
        pltpu.make_async_remote_copy(
            src_ref=sums.at[source],
            dst_ref=sums.at[source],
            send_sem=sum_send.at[d],
            recv_sem=sum_recv.at[source],
            device_id={"col": source},
            device_id_type=MESH,
        ).wait_recv()

    total = sums[0]
    for c in range(1, col_count):
        total = total + sums[c]
    factor = (rows_local * col_count) / total
    for j in range(col_blocks):
        scale[0:1, j * BLOCK:(j + 1) * BLOCK] = factor[j:j + 1, :]


def shards(row_count, col_count, left_values, left_pattern, right_values, right_pattern):
    rows_local, inner_local = left_values.shape
    inner_rows, cols_local = right_values.shape
    y_size = row_count // 2
    x_size = y_size if col_count % y_size == 0 else 1
    group = inner_local // BLOCK
    left_slots = max(1, group // 2)
    left_blocks = rows_local // BLOCK
    col_blocks = cols_local // BLOCK
    slots = col_blocks // 2
    parts = 2
    inner = row_count * inner_local
    dma = pltpu.SemaphoreType.DMA
    operands = (left_pattern.T, right_pattern, left_values, right_values)
    product, scale = pl.pallas_call(
        functools.partial(kernel, (row_count, col_count, y_size, x_size)),
        out_shape=(
            jax.ShapeDtypeStruct((rows_local, cols_local), jnp.float32),
            jax.ShapeDtypeStruct((1, cols_local), jnp.float32),
        ),
        in_specs=[pl.BlockSpec(memory_space=pltpu.HBM)] * 4,
        out_specs=(pl.BlockSpec(memory_space=pltpu.VMEM),) * 2,
        scratch_shapes=[
            pltpu.SMEM(left_pattern.shape[::-1], jnp.int32),
            pltpu.SMEM(right_pattern.shape, jnp.int32),
            pltpu.VMEM((rows_local, inner_local), jnp.bfloat16),
            pltpu.VMEM((inner_rows, cols_local), jnp.bfloat16),
            pltpu.VMEM((row_count, left_blocks, left_slots, BLOCK, BLOCK), jnp.bfloat16),
            pltpu.VMEM((col_count, slots, BLOCK, BLOCK), jnp.bfloat16),
            pltpu.VMEM((inner // (x_size * BLOCK), rows_local, x_size * BLOCK), jnp.bfloat16),
            pltpu.VMEM((col_count, col_blocks, BLOCK), jnp.float32),
            dma((4,)),
            dma((4, row_count, 1)),
            dma((row_count, 1)),
            dma((4, col_count, parts)),
            dma((col_count, parts)),
            dma((col_count,)),
            dma((col_count,)),
        ],
        compiler_params=pltpu.CompilerParams(
            collective_id=0, has_side_effects=True, vmem_limit_bytes=32 * 1024 * 1024
        ),
    )(*(pltpu.with_memory_space_constraint(x, pltpu.HBM) for x in operands))
    return product * product * scale


def solution(mesh):
    return jax.shard_map(
        functools.partial(shards, mesh.shape["row"], mesh.shape["col"]),
        mesh=mesh,
        in_specs=(P("col", "row"), P(), P("col", "row"), P()),
        out_specs=P("col", "row"),
        check_vma=False,
    )
```

```python
import functools

import jax
import jax.numpy as jnp
from jax import lax
from jax.experimental import pallas as pl
from jax.experimental.pallas import tpu as pltpu
from jax.sharding import PartitionSpec as P

BLOCK = 128
MESH = pl.DeviceIdType.MESH


class Gather:
    def __init__(self, axis, outer, inner, held, own_send, send_sem, recv_sem):
        self.axis, self.outer, self.inner = axis, outer, inner
        self.held, self.own_send, self.send_sem, self.recv_sem = held, own_send, send_sem, recv_sem
        self.parts = recv_sem.shape[1]
        self.depth = held.shape[1] // self.parts
        me = lax.axis_index(axis)
        self.me, self.o, self.i = me, me // inner, me % inner

    def copy(self, slot, part, send_sem, target):
        piece = self.held.at[slot, pl.ds(part * self.depth, self.depth)]
        return pltpu.make_async_remote_copy(
            src_ref=piece,
            dst_ref=piece,
            send_sem=send_sem,
            recv_sem=self.recv_sem.at[slot, part],
            device_id={self.axis: target},
            device_id_type=MESH,
        )

    def wait(self, slot, part):
        self.copy(slot, part, self.own_send.at[0, part], self.me).wait_recv()

    def each_inner(self, slot, part, step, act):
        target = self.i + step

        @pl.when((target >= 0) & (target < self.inner))
        def _():
            sem = self.send_sem.at[0 if step == 1 else 1, slot, part]
            act(self.copy(slot, part, sem, self.o * self.inner + target))

    def visit_own(self, act):
        for part in range(self.parts):
            for step in (1, -1):
                self.each_inner(self.me, part, step, act)
            for distance in range(1, self.outer):
                for step in (distance, -distance):
                    target = self.o + step

                    @pl.when((target >= 0) & (target < self.outer))
                    def _():
                        sem = self.own_send.at[target, part]
                        act(self.copy(self.me, part, sem, target * self.inner + self.i))

    def visit_outer(self, o, wait, act):
        slot = o * self.inner + self.i
        for part in range(self.parts):
            if wait:
                self.wait(slot, part)
            for step in (1, -1):
                self.each_inner(slot, part, step, act)

    def visit_inner(self, o, wait, act):
        for distance in range(1, self.inner):
            for step in (1, -1):
                i = self.i + step * distance

                @pl.when((i >= 0) & (i < self.inner))
                def _():
                    slot = o * self.inner + i
                    for part in range(self.parts):
                        if wait:
                            self.wait(slot, part)
                        self.each_inner(slot, part, -step, act)

    def place(self, q):
        distance = (q + 1) // 2
        sign = 2 * (q % 2) - 1
        o = self.o + sign * distance
        return o, (o >= 0) & (o < self.outer)

    def greet(self, barrier):
        count = self.outer - 1

        @pl.loop(1, self.outer)
        def _(d):
            target = ((self.o + d) % self.outer) * self.inner + self.i
            pl.semaphore_signal(barrier, inc=1, device_id={self.axis: target}, device_id_type=MESH)

        for step in (1, -1):
            there = (self.i + step >= 0) & (self.i + step < self.inner)

            @pl.when(there)
            def _():
                pl.semaphore_signal(
                    barrier, inc=1, device_id={self.axis: self.me + step}, device_id_type=MESH
                )

            count = count + jnp.where(there, 1, 0)
        return count


def start(copy):
    copy.start()


def wait_send(copy):
    copy.wait_send()


def kernel(
    sizes,
    left_ones, right_ones, left_values, right_values,
    product, scale,
    left_pattern, right_pattern, left_in, right_in, left_held, right_held, left_dense, sums,
    in_sem, left_own, left_send, left_recv, right_own, right_send, right_recv, sum_send, sum_recv,
):
    row_count, col_count, y_size, x_size = sizes
    rows_local, inner_local = left_in.shape
    left_blocks = rows_local // BLOCK
    group = inner_local // BLOCK
    left_slots = left_held.shape[2]
    col_blocks = right_in.shape[1] // BLOCK
    slots = right_held.shape[1]
    z_size = col_count // x_size
    row, col = lax.axis_index("row"), lax.axis_index("col")

    barrier = pltpu.get_barrier_semaphore()

    right = Gather("col", z_size, x_size, right_held, right_own, right_send, right_recv)
    left = Gather("row", y_size, row_count // y_size, left_held, left_own, left_send, left_recv)
    neighbours = right.greet(barrier) + left.greet(barrier)

    right_load = pltpu.make_async_copy(right_values, right_in, in_sem.at[0])
    left_load = pltpu.make_async_copy(left_values, left_in, in_sem.at[1])
    left_ones_load = pltpu.make_async_copy(left_ones, left_pattern, in_sem.at[2])
    right_ones_load = pltpu.make_async_copy(right_ones, right_pattern, in_sem.at[3])
    right_ones_load.start()
    right_load.start()
    left_ones_load.start()
    left_load.start()

    def pick(ones, wanted, candidate):
        before, found = 0, [None] * wanted
        for k, one in enumerate(ones):
            block = candidate(k)
            for s in range(min(k + 1, wanted)):
                if k == s:
                    found[s] = block
                else:
                    found[s] = jnp.where((one != 0) & (before == s), block, found[s])
            before = before + one
        return found

    def unpick(one, before, packed):
        block = jnp.zeros_like(packed[0])
        for s, value in enumerate(packed):
            block = jnp.where((one != 0) & (before == s), value, block)
        return block

    right_ones_load.wait()
    ones = [right_pattern[col, row * col_blocks + j] for j in range(col_blocks)]
    right_load.wait()
    picks = pick(ones, slots, lambda j: right_in[:, j * BLOCK:(j + 1) * BLOCK])
    for s in range(slots):
        right_held[col, s] = picks[s]
    pl.semaphore_wait(barrier, neighbours)
    right.visit_own(start)

    left_ones_load.wait()
    left_load.wait()
    for b in range(left_blocks):
        ones = [left_pattern[row * group + k, col * left_blocks + b] for k in range(group)]
        at = slice(b * BLOCK, (b + 1) * BLOCK)
        picks = pick(ones, left_slots, lambda k: left_in[at, k * BLOCK:(k + 1) * BLOCK])
        for s in range(left_slots):
            left_held[row, b, s] = picks[s]
    left.visit_own(start)

    product[...] = jnp.zeros_like(product)

    def finish_left():
        @pl.loop(1, 2 * y_size - 1)
        def _(q):
            o, valid = left.place(q)

            @pl.when(valid)
            def _():
                left.visit_outer(o, True, start)

        @pl.loop(0, y_size)
        def _(o):
            left.visit_inner(o, True, start)

        @pl.loop(0, row_count * group)
        def _(k):
            g, within = k // group, k % group
            at = pl.ds(pl.multiple_of((k % x_size) * BLOCK, BLOCK), BLOCK)
            for b in range(left_blocks):
                block_row = col * left_blocks + b
                here = left_pattern[k, block_row]
                before = 0
                for m in range(group - 1):
                    before = before + jnp.where(m < within, left_pattern[g * group + m, block_row], 0)
                left_dense[k // x_size, b * BLOCK:(b + 1) * BLOCK, at] = unpick(
                    here, before, [left_held[g, b, s] for s in range(left_slots)]
                )

    def multiply(o):
        right.visit_inner(o, True, start)
        ones, ranks = [], []
        for i in range(x_size):
            k = o * x_size + i
            line = [right_pattern[k, row * col_blocks + j] for j in range(col_blocks)]
            rank = [0] * col_blocks
            for j in range(1, col_blocks):
                rank[j] = rank[j - 1] + line[j - 1]
            ones.append(line)
            ranks.append(rank)

        def dense(i, j):
            packed = [right_held[o * x_size + i, s] for s in range(slots)]
            return unpick(ones[i][j], ranks[i][j], packed)

        for j in range(0, col_blocks, 2):
            block = jnp.concatenate(
                [jnp.concatenate([dense(i, j), dense(i, j + 1)], axis=1) for i in range(x_size)],
                axis=0,
            )
            at = pl.ds(j * BLOCK, 2 * BLOCK)
            product[:, at] += jnp.dot(left_dense[o], block, preferred_element_type=jnp.float32)

    @pl.loop(0, 2 * z_size - 1 + 2)
    def _(q):
        o, valid = right.place(q)

        @pl.when((q > 0) & valid)
        def _():
            right.visit_outer(o, True, start)

        @pl.when(q == 2)
        def _():
            finish_left()

        late, late_valid = right.place(jnp.maximum(q - 2, 0))

        @pl.when((q >= 2) & late_valid)
        def _():
            multiply(late)

    for j in range(col_blocks):
        part = product[:, j * BLOCK:(j + 1) * BLOCK]
        sums[col, j:j + 1, :] = jnp.sum(part * part, axis=0, keepdims=True)

    def sum_copy(d):
        return pltpu.make_async_remote_copy(
            src_ref=sums.at[col],
            dst_ref=sums.at[col],
            send_sem=sum_send.at[d],
            recv_sem=sum_recv.at[col],
            device_id={"col": (col + d) % col_count},
            device_id_type=MESH,
        )

    @pl.loop(1, col_count)
    def _(d):
        sum_copy(d).start()

    right.visit_own(wait_send)
    left.visit_own(wait_send)

    @pl.loop(1, 2 * y_size - 1)
    def _(q):
        o, valid = left.place(q)

        @pl.when(valid)
        def _():
            left.visit_outer(o, False, wait_send)

    @pl.loop(0, y_size)
    def _(o):
        left.visit_inner(o, False, wait_send)

    @pl.loop(1, 2 * z_size - 1)
    def _(q):
        o, valid = right.place(q)

        @pl.when(valid)
        def _():
            right.visit_outer(o, False, wait_send)

    @pl.loop(0, z_size)
    def _(o):
        right.visit_inner(o, False, wait_send)

    @pl.loop(1, col_count)
    def _(d):
        sum_copy(d).wait_send()
        source = (col + d) % col_count
        pltpu.make_async_remote_copy(
            src_ref=sums.at[source],
            dst_ref=sums.at[source],
            send_sem=sum_send.at[d],
            recv_sem=sum_recv.at[source],
            device_id={"col": source},
            device_id_type=MESH,
        ).wait_recv()

    total = sums[0]
    for c in range(1, col_count):
        total = total + sums[c]
    factor = (rows_local * col_count) / total
    for j in range(col_blocks):
        scale[0:1, j * BLOCK:(j + 1) * BLOCK] = factor[j:j + 1, :]


def shards(row_count, col_count, left_values, left_pattern, right_values, right_pattern):
    rows_local, inner_local = left_values.shape
    inner_rows, cols_local = right_values.shape
    y_size = row_count // 2
    x_size = y_size if col_count % y_size == 0 else 1
    group = inner_local // BLOCK
    left_slots = max(1, group // 2)
    left_blocks = rows_local // BLOCK
    col_blocks = cols_local // BLOCK
    slots = col_blocks // 2
    parts = 2
    inner = row_count * inner_local
    dma = pltpu.SemaphoreType.DMA
    operands = (left_pattern.T, right_pattern, left_values, right_values)
    product, scale = pl.pallas_call(
        functools.partial(kernel, (row_count, col_count, y_size, x_size)),
        out_shape=(
            jax.ShapeDtypeStruct((rows_local, cols_local), jnp.float32),
            jax.ShapeDtypeStruct((1, cols_local), jnp.float32),
        ),
        in_specs=[pl.BlockSpec(memory_space=pltpu.HBM)] * 4,
        out_specs=(pl.BlockSpec(memory_space=pltpu.VMEM),) * 2,
        scratch_shapes=[
            pltpu.SMEM(left_pattern.shape[::-1], jnp.int32),
            pltpu.SMEM(right_pattern.shape, jnp.int32),
            pltpu.VMEM((rows_local, inner_local), jnp.bfloat16),
            pltpu.VMEM((inner_rows, cols_local), jnp.bfloat16),
            pltpu.VMEM((row_count, left_blocks, left_slots, BLOCK, BLOCK), jnp.bfloat16),
            pltpu.VMEM((col_count, slots, BLOCK, BLOCK), jnp.bfloat16),
            pltpu.VMEM((inner // (x_size * BLOCK), rows_local, x_size * BLOCK), jnp.bfloat16),
            pltpu.VMEM((col_count, col_blocks, BLOCK), jnp.float32),
            dma((4,)),
            dma((y_size, 1)),
            dma((2, row_count, 1)),
            dma((row_count, 1)),
            dma((col_count // x_size, parts)),
            dma((2, col_count, parts)),
            dma((col_count, parts)),
            dma((col_count,)),
            dma((col_count,)),
        ],
        compiler_params=pltpu.CompilerParams(
            collective_id=0, has_side_effects=True, vmem_limit_bytes=32 * 1024 * 1024
        ),
    )(*(pltpu.with_memory_space_constraint(x, pltpu.HBM) for x in operands))
    return product * product * scale


def solution(mesh):
    return jax.shard_map(
        functools.partial(shards, mesh.shape["row"], mesh.shape["col"]),
        mesh=mesh,
        in_specs=(P("col", "row"), P(), P("col", "row"), P()),
        out_specs=P("col", "row"),
        check_vma=False,
    )
```

```python
import functools

import jax
import jax.numpy as jnp
from jax import lax
from jax.experimental import pallas as pl
from jax.experimental.pallas import tpu as pltpu
from jax.sharding import PartitionSpec as P

BLOCK = 128
MESH = pl.DeviceIdType.MESH


class Gather:
    def __init__(self, axis, outer, inner, held, own_send, send_sem, recv_sem):
        self.axis, self.outer, self.inner = axis, outer, inner
        self.held, self.own_send, self.send_sem, self.recv_sem = held, own_send, send_sem, recv_sem
        self.parts = recv_sem.shape[1]
        self.depth = held.shape[1] // self.parts
        me = lax.axis_index(axis)
        self.me, self.o, self.i = me, me // inner, me % inner

    def copy(self, slot, part, send_sem, target):
        piece = self.held.at[slot, pl.ds(part * self.depth, self.depth)]
        return pltpu.make_async_remote_copy(
            src_ref=piece,
            dst_ref=piece,
            send_sem=send_sem,
            recv_sem=self.recv_sem.at[slot, part],
            device_id={self.axis: target},
            device_id_type=MESH,
        )

    def wait(self, slot, part):
        self.copy(slot, part, self.own_send.at[0, part], self.me).wait_recv()

    def each_inner(self, slot, part, step, act):
        target = self.i + step

        @pl.when((target >= 0) & (target < self.inner))
        def _():
            sem = self.send_sem.at[0 if step == 1 else 1, slot, part]
            act(self.copy(slot, part, sem, self.o * self.inner + target))

    def visit_own(self, act):
        for part in range(self.parts):
            for step in (1, -1):
                self.each_inner(self.me, part, step, act)
            for distance in range(1, self.outer):
                for step in (distance, -distance):
                    target = self.o + step

                    @pl.when((target >= 0) & (target < self.outer))
                    def _():
                        sem = self.own_send.at[target, part]
                        act(self.copy(self.me, part, sem, target * self.inner + self.i))

    def visit_outer(self, o, wait, act):
        slot = o * self.inner + self.i
        for part in range(self.parts):
            if wait:
                self.wait(slot, part)
            for step in (1, -1):
                self.each_inner(slot, part, step, act)

    def visit_inner(self, o, wait, act):
        for distance in range(1, self.inner):
            for step in (1, -1):
                i = self.i + step * distance

                @pl.when((i >= 0) & (i < self.inner))
                def _():
                    slot = o * self.inner + i
                    for part in range(self.parts):
                        if wait:
                            self.wait(slot, part)
                        self.each_inner(slot, part, -step, act)

    def place(self, q):
        distance = (q + 1) // 2
        sign = 2 * (q % 2) - 1
        o = self.o + sign * distance
        return o, (o >= 0) & (o < self.outer)

    def greet(self, barrier):
        count = self.outer - 1

        @pl.loop(1, self.outer)
        def _(d):
            target = ((self.o + d) % self.outer) * self.inner + self.i
            pl.semaphore_signal(barrier, inc=1, device_id={self.axis: target}, device_id_type=MESH)

        for step in (1, -1):
            there = (self.i + step >= 0) & (self.i + step < self.inner)

            @pl.when(there)
            def _():
                pl.semaphore_signal(
                    barrier, inc=1, device_id={self.axis: self.me + step}, device_id_type=MESH
                )

            count = count + jnp.where(there, 1, 0)
        return count


def start(copy):
    copy.start()


def wait_send(copy):
    copy.wait_send()


def kernel(
    sizes,
    left_ones, right_ones, left_values, right_values,
    product, scale,
    left_pattern, right_pattern, left_in, right_in, left_held, right_held, left_dense, stage, sums,
    ones_sem, left_sem, right_sem, left_own, left_send, left_recv, right_own, right_send, right_recv, sum_send, sum_recv,
):
    row_count, col_count, y_size, x_size = sizes
    left_blocks, group = left_in.shape[:2]
    rows_local = left_blocks * BLOCK
    left_slots = left_held.shape[2]
    col_blocks = right_in.shape[0]
    slots = right_held.shape[1]
    z_size = col_count // x_size
    row, col = lax.axis_index("row"), lax.axis_index("col")

    barrier = pltpu.get_barrier_semaphore()

    right = Gather("col", z_size, x_size, right_held, right_own, right_send, right_recv)
    left = Gather("row", y_size, row_count // y_size, left_held, left_own, left_send, left_recv)
    neighbours = right.greet(barrier) + left.greet(barrier)

    left_ones_load = pltpu.make_async_copy(left_ones, left_pattern, ones_sem.at[0])
    right_ones_load = pltpu.make_async_copy(right_ones, right_pattern, ones_sem.at[1])
    left_ones_load.start()
    right_ones_load.start()
    loads = []
    for b in range(left_blocks):
        for k in range(group):
            source = left_values.at[pl.ds(b * BLOCK, BLOCK), pl.ds(k * BLOCK, BLOCK)]
            loads.append(pltpu.make_async_copy(source, left_in.at[b, k], left_sem.at[b, k]))
    right_loads = []
    for j in range(col_blocks):
        source = right_values.at[:, pl.ds(j * BLOCK, BLOCK)]
        right_loads.append(pltpu.make_async_copy(source, right_in.at[j], right_sem.at[j]))
    for load in loads + right_loads:
        load.start()
    stage[:, slots] = jnp.zeros(stage.shape[:1] + stage.shape[2:], stage.dtype)

    def chosen(ones, wanted):
        found = [0] * wanted
        count = 0
        for k, one in enumerate(ones):
            for s in range(min(k + 1, wanted)):
                found[s] = jnp.where((one != 0) & (count == s), k, found[s])
            count = count + one
        return found

    def unpick(one, before, packed):
        block = jnp.zeros_like(packed[0])
        for s, value in enumerate(packed):
            block = jnp.where((one != 0) & (before == s), value, block)
        return block

    left_ones_load.wait()
    for load in loads:
        load.wait()
    for b in range(left_blocks):
        ones = [left_pattern[row * group + k, col * left_blocks + b] for k in range(group)]
        picks = chosen(ones, left_slots)
        for s in range(left_slots):
            left_held[row, b, s] = left_in[b, picks[s]]
    pl.semaphore_wait(barrier, neighbours)
    left.visit_own(start)

    right_ones_load.wait()
    picks = chosen([right_pattern[col, row * col_blocks + j] for j in range(col_blocks)], slots)
    for load in right_loads:
        load.wait()
    for s in range(slots):
        right_held[col, s] = right_in[picks[s]]
    right.visit_own(start)

    product[...] = jnp.zeros_like(product)

    def finish_left():
        @pl.loop(1, 2 * y_size - 1)
        def _(q):
            o, valid = left.place(q)

            @pl.when(valid)
            def _():
                left.visit_outer(o, True, start)

        @pl.loop(0, y_size)
        def _(o):
            left.visit_inner(o, True, start)

        @pl.loop(0, row_count * group)
        def _(k):
            g, within = k // group, k % group
            at = pl.ds(pl.multiple_of((k % x_size) * BLOCK, BLOCK), BLOCK)
            for b in range(left_blocks):
                block_row = col * left_blocks + b
                here = left_pattern[k, block_row]
                before = 0
                for m in range(group - 1):
                    before = before + jnp.where(m < within, left_pattern[g * group + m, block_row], 0)
                left_dense[k // x_size, b * BLOCK:(b + 1) * BLOCK, at] = unpick(
                    here, before, [left_held[g, b, s] for s in range(left_slots)]
                )

    def multiply(o):
        right.visit_inner(o, True, start)
        index = []
        for i in range(x_size):
            k = o * x_size + i
            stage[i, :slots] = right_held[k]
            count, line = 0, []
            for j in range(col_blocks):
                one = right_pattern[k, row * col_blocks + j]
                line.append(jnp.where(one != 0, count, slots))
                count = count + one
            index.append(line)

        def dense(i, j):
            return stage[i, index[i][j]]

        for j in range(0, col_blocks, 2):
            block = jnp.concatenate(
                [jnp.concatenate([dense(i, j), dense(i, j + 1)], axis=1) for i in range(x_size)],
                axis=0,
            )
            at = pl.ds(j * BLOCK, 2 * BLOCK)
            product[:, at] += jnp.dot(left_dense[o], block, preferred_element_type=jnp.float32)

    @pl.loop(0, 2 * z_size - 1 + 2)
    def _(q):
        o, valid = right.place(q)

        @pl.when((q > 0) & valid)
        def _():
            right.visit_outer(o, True, start)

        @pl.when(q == 2)
        def _():
            finish_left()

        late, late_valid = right.place(jnp.maximum(q - 2, 0))

        @pl.when((q >= 2) & late_valid)
        def _():
            multiply(late)

    for j in range(col_blocks):
        part = product[:, j * BLOCK:(j + 1) * BLOCK]
        sums[col, j:j + 1, :] = jnp.sum(part * part, axis=0, keepdims=True)

    def sum_copy(d):
        return pltpu.make_async_remote_copy(
            src_ref=sums.at[col],
            dst_ref=sums.at[col],
            send_sem=sum_send.at[d],
            recv_sem=sum_recv.at[col],
            device_id={"col": (col + d) % col_count},
            device_id_type=MESH,
        )

    @pl.loop(1, col_count)
    def _(d):
        sum_copy(d).start()

    right.visit_own(wait_send)
    left.visit_own(wait_send)

    @pl.loop(1, 2 * y_size - 1)
    def _(q):
        o, valid = left.place(q)

        @pl.when(valid)
        def _():
            left.visit_outer(o, False, wait_send)

    @pl.loop(0, y_size)
    def _(o):
        left.visit_inner(o, False, wait_send)

    @pl.loop(1, 2 * z_size - 1)
    def _(q):
        o, valid = right.place(q)

        @pl.when(valid)
        def _():
            right.visit_outer(o, False, wait_send)

    @pl.loop(0, z_size)
    def _(o):
        right.visit_inner(o, False, wait_send)

    @pl.loop(1, col_count)
    def _(d):
        sum_copy(d).wait_send()
        source = (col + d) % col_count
        pltpu.make_async_remote_copy(
            src_ref=sums.at[source],
            dst_ref=sums.at[source],
            send_sem=sum_send.at[d],
            recv_sem=sum_recv.at[source],
            device_id={"col": source},
            device_id_type=MESH,
        ).wait_recv()

    total = sums[0]
    for c in range(1, col_count):
        total = total + sums[c]
    factor = (rows_local * col_count) / total
    for j in range(col_blocks):
        scale[0:1, j * BLOCK:(j + 1) * BLOCK] = factor[j:j + 1, :]


def shards(row_count, col_count, left_values, left_pattern, right_values, right_pattern):
    rows_local, inner_local = left_values.shape
    inner_rows, cols_local = right_values.shape
    y_size = row_count // 2
    x_size = y_size if col_count % y_size == 0 else 1
    group = inner_local // BLOCK
    left_slots = max(1, group // 2)
    left_blocks = rows_local // BLOCK
    col_blocks = cols_local // BLOCK
    slots = col_blocks // 2
    parts = 2
    inner = row_count * inner_local
    dma = pltpu.SemaphoreType.DMA
    operands = (left_pattern.T, right_pattern, left_values, right_values)
    product, scale = pl.pallas_call(
        functools.partial(kernel, (row_count, col_count, y_size, x_size)),
        out_shape=(
            jax.ShapeDtypeStruct((rows_local, cols_local), jnp.float32),
            jax.ShapeDtypeStruct((1, cols_local), jnp.float32),
        ),
        in_specs=[pl.BlockSpec(memory_space=pltpu.HBM)] * 4,
        out_specs=(pl.BlockSpec(memory_space=pltpu.VMEM),) * 2,
        scratch_shapes=[
            pltpu.SMEM(left_pattern.shape[::-1], jnp.int32),
            pltpu.SMEM(right_pattern.shape, jnp.int32),
            pltpu.VMEM((left_blocks, group, BLOCK, BLOCK), jnp.bfloat16),
            pltpu.VMEM((col_blocks, BLOCK, BLOCK), jnp.bfloat16),
            pltpu.VMEM((row_count, left_blocks, left_slots, BLOCK, BLOCK), jnp.bfloat16),
            pltpu.VMEM((col_count, slots, BLOCK, BLOCK), jnp.bfloat16),
            pltpu.VMEM((inner // (x_size * BLOCK), rows_local, x_size * BLOCK), jnp.bfloat16),
            pltpu.VMEM((x_size, slots + 1, BLOCK, BLOCK), jnp.bfloat16),
            pltpu.VMEM((col_count, col_blocks, BLOCK), jnp.float32),
            dma((2,)),
            dma((left_blocks, group)),
            dma((col_blocks,)),
            dma((y_size, 1)),
            dma((2, row_count, 1)),
            dma((row_count, 1)),
            dma((col_count // x_size, parts)),
            dma((2, col_count, parts)),
            dma((col_count, parts)),
            dma((col_count,)),
            dma((col_count,)),
        ],
        compiler_params=pltpu.CompilerParams(
            collective_id=0, has_side_effects=True, vmem_limit_bytes=32 * 1024 * 1024
        ),
    )(*(pltpu.with_memory_space_constraint(x, pltpu.HBM) for x in operands))
    return product * product * scale


def solution(mesh):
    return jax.shard_map(
        functools.partial(shards, mesh.shape["row"], mesh.shape["col"]),
        mesh=mesh,
        in_specs=(P("col", "row"), P(), P("col", "row"), P()),
        out_specs=P("col", "row"),
        check_vma=False,
    )
```

```python
import functools

import jax
import jax.numpy as jnp
from jax import lax
from jax.experimental import pallas as pl
from jax.experimental.pallas import tpu as pltpu
from jax.sharding import PartitionSpec as P

BLOCK = 128
MESH = pl.DeviceIdType.MESH


class Gather:
    def __init__(self, axis, outer, inner, held, send_sem, recv_sem):
        self.axis, self.outer, self.inner = axis, outer, inner
        self.held, self.send_sem, self.recv_sem = held, send_sem, recv_sem
        self.parts = recv_sem.shape[1]
        self.depth = held.shape[1] // self.parts
        me = lax.axis_index(axis)
        self.me, self.o, self.i = me, me // inner, me % inner

    def copy(self, slot, part, lane, target):
        piece = self.held.at[slot, pl.ds(part * self.depth, self.depth)]
        return pltpu.make_async_remote_copy(
            src_ref=piece,
            dst_ref=piece,
            send_sem=self.send_sem.at[lane, slot, part],
            recv_sem=self.recv_sem.at[slot, part],
            device_id={self.axis: target},
            device_id_type=MESH,
        )

    def each_outer(self, slot, part, step, act):
        target = self.o + step

        @pl.when((target >= 0) & (target < self.outer))
        def _():
            act(self.copy(slot, part, 0 if step == 1 else 1, target * self.inner + self.i))

    def each_inner(self, slot, part, step, act):
        target = self.i + step

        @pl.when((target >= 0) & (target < self.inner))
        def _():
            act(self.copy(slot, part, 2 if step == 1 else 3, self.o * self.inner + target))

    def visit_own(self, act):
        for part in range(self.parts):
            for step in (1, -1):
                self.each_outer(self.me, part, step, act)
            for step in (1, -1):
                self.each_inner(self.me, part, step, act)

    def visit_outer(self, distance, wait, act):
        for part in range(self.parts):
            for sign in (-1, 1):
                o = self.o + sign * distance

                @pl.when((o >= 0) & (o < self.outer))
                def _():
                    slot = o * self.inner + self.i
                    if wait:
                        self.copy(slot, part, 0, self.me).wait_recv()
                    self.each_outer(slot, part, -sign, act)
                    for step in (1, -1):
                        self.each_inner(slot, part, step, act)

    def visit_inner(self, o, wait, act):
        for distance in range(1, self.inner):
            for step in (1, -1):
                i = self.i + step * distance

                @pl.when((i >= 0) & (i < self.inner))
                def _():
                    slot = o * self.inner + i
                    for part in range(self.parts):
                        if wait:
                            self.copy(slot, part, 0, self.me).wait_recv()
                        self.each_inner(slot, part, -step, act)

    def greet(self, barrier):
        count = 0
        for step in (1, -1):
            for own, size, stride in ((self.o, self.outer, self.inner), (self.i, self.inner, 1)):
                there = (own + step >= 0) & (own + step < size)

                @pl.when(there)
                def _():
                    pl.semaphore_signal(
                        barrier, inc=1, device_id={self.axis: self.me + step * stride}, device_id_type=MESH
                    )

                count = count + jnp.where(there, 1, 0)
        return count


def start(copy):
    copy.start()


def wait_send(copy):
    copy.wait_send()


def kernel(
    sizes,
    left_ones, right_ones, left_values, right_values,
    product, scale,
    left_pattern, right_pattern, left_in, right_in, left_held, right_held, left_dense, sums,
    in_sem, left_send, left_recv, right_send, right_recv, sum_send, sum_recv,
):
    row_count, col_count, y_size, x_size = sizes
    rows_local, inner_local = left_in.shape
    left_blocks = rows_local // BLOCK
    group = inner_local // BLOCK
    left_slots = left_held.shape[2]
    col_blocks = right_in.shape[1] // BLOCK
    slots = right_held.shape[1]
    z_size = col_count // x_size
    row, col = lax.axis_index("row"), lax.axis_index("col")

    barrier = pltpu.get_barrier_semaphore()

    right = Gather("col", z_size, x_size, right_held, right_send, right_recv)
    left = Gather("row", y_size, row_count // y_size, left_held, left_send, left_recv)
    neighbours = right.greet(barrier) + left.greet(barrier)

    right_load = pltpu.make_async_copy(right_values, right_in, in_sem.at[0])
    left_load = pltpu.make_async_copy(left_values, left_in, in_sem.at[1])
    left_ones_load = pltpu.make_async_copy(left_ones, left_pattern, in_sem.at[2])
    right_ones_load = pltpu.make_async_copy(right_ones, right_pattern, in_sem.at[3])
    left_ones_load.start()
    right_ones_load.start()
    left_load.start()
    right_load.start()

    def pick(ones, wanted, candidate):
        before, found = 0, [None] * wanted
        for k, one in enumerate(ones):
            block = candidate(k)
            for s in range(min(k + 1, wanted)):
                if k == s:
                    found[s] = block
                else:
                    found[s] = jnp.where((one != 0) & (before == s), block, found[s])
            before = before + one
        return found

    def unpick(one, before, packed):
        block = jnp.zeros_like(packed[0])
        for s, value in enumerate(packed):
            block = jnp.where((one != 0) & (before == s), value, block)
        return block

    left_ones_load.wait()
    left_load.wait()
    for b in range(left_blocks):
        ones = [left_pattern[row * group + k, col * left_blocks + b] for k in range(group)]
        at = slice(b * BLOCK, (b + 1) * BLOCK)
        picks = pick(ones, left_slots, lambda k: left_in[at, k * BLOCK:(k + 1) * BLOCK])
        for s in range(left_slots):
            left_held[row, b, s] = picks[s]
    pl.semaphore_wait(barrier, neighbours)
    left.visit_own(start)

    right_ones_load.wait()
    ones = [right_pattern[col, row * col_blocks + j] for j in range(col_blocks)]
    right_load.wait()
    picks = pick(ones, slots, lambda j: right_in[:, j * BLOCK:(j + 1) * BLOCK])
    for s in range(slots):
        right_held[col, s] = picks[s]
    right.visit_own(start)

    product[...] = jnp.zeros_like(product)

    def finish_left():
        @pl.loop(1, y_size)
        def _(distance):
            left.visit_outer(distance, True, start)

        @pl.loop(0, y_size)
        def _(o):
            left.visit_inner(o, True, start)

        @pl.loop(0, row_count * group)
        def _(k):
            g, within = k // group, k % group
            at = pl.ds(pl.multiple_of((k % x_size) * BLOCK, BLOCK), BLOCK)
            for b in range(left_blocks):
                block_row = col * left_blocks + b
                here = left_pattern[k, block_row]
                before = 0
                for m in range(group - 1):
                    before = before + jnp.where(m < within, left_pattern[g * group + m, block_row], 0)
                left_dense[k // x_size, b * BLOCK:(b + 1) * BLOCK, at] = unpick(
                    here, before, [left_held[g, b, s] for s in range(left_slots)]
                )

    def multiply(o):
        right.visit_inner(o, True, start)
        ones, ranks = [], []
        for i in range(x_size):
            k = o * x_size + i
            line = [right_pattern[k, row * col_blocks + j] for j in range(col_blocks)]
            rank = [0] * col_blocks
            for j in range(1, col_blocks):
                rank[j] = rank[j - 1] + line[j - 1]
            ones.append(line)
            ranks.append(rank)

        def dense(i, j):
            packed = [right_held[o * x_size + i, s] for s in range(slots)]
            return unpick(ones[i][j], ranks[i][j], packed)

        for j in range(0, col_blocks, 2):
            block = jnp.concatenate(
                [jnp.concatenate([dense(i, j), dense(i, j + 1)], axis=1) for i in range(x_size)],
                axis=0,
            )
            at = pl.ds(j * BLOCK, 2 * BLOCK)
            product[:, at] += jnp.dot(left_dense[o], block, preferred_element_type=jnp.float32)

    lag = jnp.where((right.o > 0) & (right.o < z_size - 1), 2, 1)

    @pl.loop(1, z_size + 2)
    def _(t):
        @pl.when(t < z_size)
        def _():
            right.visit_outer(t, True, start)

        @pl.when(t == lag)
        def _():
            finish_left()

        @pl.loop(0, 2)
        def _(side):
            distance = t - lag
            o = right.o + (2 * side - 1) * distance

            @pl.when((distance >= 0) & (distance + side > 0) & (o >= 0) & (o < z_size))
            def _():
                multiply(o)

    for j in range(col_blocks):
        part = product[:, j * BLOCK:(j + 1) * BLOCK]
        sums[col, j:j + 1, :] = jnp.sum(part * part, axis=0, keepdims=True)

    def sum_copy(d):
        return pltpu.make_async_remote_copy(
            src_ref=sums.at[col],
            dst_ref=sums.at[col],
            send_sem=sum_send.at[d],
            recv_sem=sum_recv.at[col],
            device_id={"col": (col + d) % col_count},
            device_id_type=MESH,
        )

    @pl.loop(1, col_count)
    def _(d):
        sum_copy(d).start()

    right.visit_own(wait_send)
    left.visit_own(wait_send)

    @pl.loop(1, y_size)
    def _(distance):
        left.visit_outer(distance, False, wait_send)

    @pl.loop(0, y_size)
    def _(o):
        left.visit_inner(o, False, wait_send)

    @pl.loop(1, z_size)
    def _(distance):
        right.visit_outer(distance, False, wait_send)

    @pl.loop(0, z_size)
    def _(o):
        right.visit_inner(o, False, wait_send)

    @pl.loop(1, col_count)
    def _(d):
        sum_copy(d).wait_send()
        source = (col + d) % col_count
        pltpu.make_async_remote_copy(
            src_ref=sums.at[source],
            dst_ref=sums.at[source],
            send_sem=sum_send.at[d],
            recv_sem=sum_recv.at[source],
            device_id={"col": source},
            device_id_type=MESH,
        ).wait_recv()

    total = sums[0]
    for c in range(1, col_count):
        total = total + sums[c]
    factor = (rows_local * col_count) / total
    for j in range(col_blocks):
        scale[0:1, j * BLOCK:(j + 1) * BLOCK] = factor[j:j + 1, :]


def shards(row_count, col_count, left_values, left_pattern, right_values, right_pattern):
    rows_local, inner_local = left_values.shape
    inner_rows, cols_local = right_values.shape
    y_size = row_count // 2
    x_size = y_size if col_count % y_size == 0 else 1
    group = inner_local // BLOCK
    left_slots = max(1, group // 2)
    left_blocks = rows_local // BLOCK
    col_blocks = cols_local // BLOCK
    slots = col_blocks // 2
    parts = 2
    inner = row_count * inner_local
    dma = pltpu.SemaphoreType.DMA
    operands = (left_pattern.T, right_pattern, left_values, right_values)
    product, scale = pl.pallas_call(
        functools.partial(kernel, (row_count, col_count, y_size, x_size)),
        out_shape=(
            jax.ShapeDtypeStruct((rows_local, cols_local), jnp.float32),
            jax.ShapeDtypeStruct((1, cols_local), jnp.float32),
        ),
        in_specs=[pl.BlockSpec(memory_space=pltpu.HBM)] * 4,
        out_specs=(pl.BlockSpec(memory_space=pltpu.VMEM),) * 2,
        scratch_shapes=[
            pltpu.SMEM(left_pattern.shape[::-1], jnp.int32),
            pltpu.SMEM(right_pattern.shape, jnp.int32),
            pltpu.VMEM((rows_local, inner_local), jnp.bfloat16),
            pltpu.VMEM((inner_rows, cols_local), jnp.bfloat16),
            pltpu.VMEM((row_count, left_blocks, left_slots, BLOCK, BLOCK), jnp.bfloat16),
            pltpu.VMEM((col_count, slots, BLOCK, BLOCK), jnp.bfloat16),
            pltpu.VMEM((inner // (x_size * BLOCK), rows_local, x_size * BLOCK), jnp.bfloat16),
            pltpu.VMEM((col_count, col_blocks, BLOCK), jnp.float32),
            dma((4,)),
            dma((4, row_count, 1)),
            dma((row_count, 1)),
            dma((4, col_count, parts)),
            dma((col_count, parts)),
            dma((col_count,)),
            dma((col_count,)),
        ],
        compiler_params=pltpu.CompilerParams(
            collective_id=0, has_side_effects=True, vmem_limit_bytes=32 * 1024 * 1024
        ),
    )(*(pltpu.with_memory_space_constraint(x, pltpu.HBM) for x in operands))
    return product * product * scale


def solution(mesh):
    return jax.shard_map(
        functools.partial(shards, mesh.shape["row"], mesh.shape["col"]),
        mesh=mesh,
        in_specs=(P("col", "row"), P(), P("col", "row"), P()),
        out_specs=P("col", "row"),
        check_vma=False,
    )
```

```python
import functools

import jax
import jax.numpy as jnp
from jax import lax
from jax.experimental import pallas as pl
from jax.experimental.pallas import tpu as pltpu
from jax.sharding import PartitionSpec as P

BLOCK = 128
SCALE_STEPS = 8
MESH = pl.DeviceIdType.MESH


class Gather:
    def __init__(self, axis, outer, inner, held, send_sem, recv_sem):
        self.axis, self.outer, self.inner = axis, outer, inner
        self.held, self.send_sem, self.recv_sem = held, send_sem, recv_sem
        self.parts = recv_sem.shape[1]
        self.depth = held.shape[1] // self.parts
        me = lax.axis_index(axis)
        self.me, self.o, self.i = me, me // inner, me % inner

    def copy(self, slot, part, lane, target):
        piece = self.held.at[slot, pl.ds(part * self.depth, self.depth)]
        return pltpu.make_async_remote_copy(
            src_ref=piece,
            dst_ref=piece,
            send_sem=self.send_sem.at[lane, slot, part],
            recv_sem=self.recv_sem.at[slot, part],
            device_id={self.axis: target},
            device_id_type=MESH,
        )

    def each_outer(self, slot, part, step, act):
        target = self.o + step

        @pl.when((target >= 0) & (target < self.outer))
        def _():
            act(self.copy(slot, part, 0 if step == 1 else 1, target * self.inner + self.i))

    def each_inner(self, slot, part, step, act):
        target = self.i + step

        @pl.when((target >= 0) & (target < self.inner))
        def _():
            act(self.copy(slot, part, 2 if step == 1 else 3, self.o * self.inner + target))

    def visit_own(self, act):
        for part in range(self.parts):
            for step in (1, -1):
                self.each_outer(self.me, part, step, act)
            for step in (1, -1):
                self.each_inner(self.me, part, step, act)

    def visit_outer(self, distance, wait, act):
        for part in range(self.parts):
            for sign in (-1, 1):
                o = self.o + sign * distance

                @pl.when((o >= 0) & (o < self.outer))
                def _():
                    slot = o * self.inner + self.i
                    if wait:
                        self.copy(slot, part, 0, self.me).wait_recv()
                    self.each_outer(slot, part, -sign, act)
                    for step in (1, -1):
                        self.each_inner(slot, part, step, act)

    def visit_inner(self, o, wait, act):
        for distance in range(1, self.inner):
            for step in (1, -1):
                i = self.i + step * distance

                @pl.when((i >= 0) & (i < self.inner))
                def _():
                    slot = o * self.inner + i
                    for part in range(self.parts):
                        if wait:
                            self.copy(slot, part, 0, self.me).wait_recv()
                        self.each_inner(slot, part, -step, act)

    def greet(self, barrier):
        count = 0
        for step in (1, -1):
            for own, size, stride in ((self.o, self.outer, self.inner), (self.i, self.inner, 1)):
                there = (own + step >= 0) & (own + step < size)

                @pl.when(there)
                def _():
                    pl.semaphore_signal(
                        barrier, inc=1, device_id={self.axis: self.me + step * stride}, device_id_type=MESH
                    )

                count = count + jnp.where(there, 1, 0)
        return count


def start(copy):
    copy.start()


def wait_send(copy):
    copy.wait_send()


def kernel(
    sizes,
    left_ones, right_ones, left_values, right_values,
    product, scale,
    left_pattern, right_pattern, left_in, right_in, left_held, right_held, left_dense, sums,
    in_sem, left_send, left_recv, right_send, right_recv, sum_send, sum_recv,
):
    row_count, col_count, y_size, x_size = sizes
    rows_local, inner_local = left_in.shape
    left_blocks = rows_local // BLOCK
    group = inner_local // BLOCK
    left_slots = left_held.shape[2]
    col_blocks = right_in.shape[1] // BLOCK
    slots = right_held.shape[1]
    z_size = col_count // x_size
    row, col = lax.axis_index("row"), lax.axis_index("col")

    barrier = pltpu.get_barrier_semaphore()

    right = Gather("col", z_size, x_size, right_held, right_send, right_recv)
    left = Gather("row", y_size, row_count // y_size, left_held, left_send, left_recv)
    neighbours = right.greet(barrier) + left.greet(barrier)

    right_load = pltpu.make_async_copy(right_values, right_in, in_sem.at[0])
    left_load = pltpu.make_async_copy(left_values, left_in, in_sem.at[1])
    left_ones_load = pltpu.make_async_copy(left_ones, left_pattern, in_sem.at[2])
    right_ones_load = pltpu.make_async_copy(right_ones, right_pattern, in_sem.at[3])
    left_ones_load.start()
    right_ones_load.start()
    left_load.start()
    right_load.start()

    def pick(ones, wanted, candidate):
        before, found = 0, [None] * wanted
        for k, one in enumerate(ones):
            block = candidate(k)
            for s in range(min(k + 1, wanted)):
                if k == s:
                    found[s] = block
                else:
                    found[s] = jnp.where((one != 0) & (before == s), block, found[s])
            before = before + one
        return found

    def unpick(one, before, packed):
        block = jnp.zeros_like(packed[0])
        for s, value in enumerate(packed):
            block = jnp.where((one != 0) & (before == s), value, block)
        return block

    left_ones_load.wait()
    left_load.wait()
    for b in range(left_blocks):
        ones = [left_pattern[row * group + k, col * left_blocks + b] for k in range(group)]
        at = slice(b * BLOCK, (b + 1) * BLOCK)
        picks = pick(ones, left_slots, lambda k: left_in[at, k * BLOCK:(k + 1) * BLOCK])
        for s in range(left_slots):
            left_held[row, b, s] = picks[s]
    pl.semaphore_wait(barrier, neighbours)
    left.visit_own(start)

    right_ones_load.wait()
    ones = [right_pattern[col, row * col_blocks + j] for j in range(col_blocks)]
    right_load.wait()
    picks = pick(ones, slots, lambda j: right_in[:, j * BLOCK:(j + 1) * BLOCK])
    for s in range(slots):
        right_held[col, s] = picks[s]
    right.visit_own(start)

    product[...] = jnp.zeros_like(product)

    def finish_left():
        @pl.loop(1, y_size)
        def _(distance):
            left.visit_outer(distance, True, start)

        @pl.loop(0, y_size)
        def _(o):
            left.visit_inner(o, True, start)

        @pl.loop(0, row_count * group)
        def _(k):
            g, within = k // group, k % group
            at = pl.ds(pl.multiple_of((k % x_size) * BLOCK, BLOCK), BLOCK)
            for b in range(left_blocks):
                block_row = col * left_blocks + b
                here = left_pattern[k, block_row]
                before = 0
                for m in range(group - 1):
                    before = before + jnp.where(m < within, left_pattern[g * group + m, block_row], 0)
                left_dense[k // x_size, b * BLOCK:(b + 1) * BLOCK, at] = unpick(
                    here, before, [left_held[g, b, s] for s in range(left_slots)]
                )

    def multiply(o):
        right.visit_inner(o, True, start)
        ones, ranks = [], []
        for i in range(x_size):
            k = o * x_size + i
            line = [right_pattern[k, row * col_blocks + j] for j in range(col_blocks)]
            rank = [0] * col_blocks
            for j in range(1, col_blocks):
                rank[j] = rank[j - 1] + line[j - 1]
            ones.append(line)
            ranks.append(rank)

        def dense(i, j):
            packed = [right_held[o * x_size + i, s] for s in range(slots)]
            return unpick(ones[i][j], ranks[i][j], packed)

        for j in range(0, col_blocks, 2):
            block = jnp.concatenate(
                [jnp.concatenate([dense(i, j), dense(i, j + 1)], axis=1) for i in range(x_size)],
                axis=0,
            )
            at = pl.ds(j * BLOCK, 2 * BLOCK)
            product[:, at] += jnp.dot(left_dense[o], block, preferred_element_type=jnp.float32)

    lag = jnp.where((right.o > 0) & (right.o < z_size - 1), 2, 1)

    @pl.loop(1, z_size + 2)
    def _(t):
        @pl.when(t < z_size)
        def _():
            right.visit_outer(t, True, start)

        @pl.when(t == lag)
        def _():
            finish_left()

        @pl.loop(0, 2)
        def _(side):
            distance = t - lag
            o = right.o + (2 * side - 1) * distance

            @pl.when((distance >= 0) & (distance + side > 0) & (o >= 0) & (o < z_size))
            def _():
                multiply(o)

    for j in range(col_blocks):
        part = product[:, j * BLOCK:(j + 1) * BLOCK]
        sums[col, j:j + 1, :] = jnp.sum(part * part, axis=0, keepdims=True)

    def sum_copy(d):
        return pltpu.make_async_remote_copy(
            src_ref=sums.at[col],
            dst_ref=sums.at[col],
            send_sem=sum_send.at[d],
            recv_sem=sum_recv.at[col],
            device_id={"col": (col + d) % col_count},
            device_id_type=MESH,
        )

    @pl.loop(1, col_count)
    def _(d):
        sum_copy(d).start()

    right.visit_own(wait_send)
    left.visit_own(wait_send)

    @pl.loop(1, y_size)
    def _(distance):
        left.visit_outer(distance, False, wait_send)

    @pl.loop(0, y_size)
    def _(o):
        left.visit_inner(o, False, wait_send)

    @pl.loop(1, z_size)
    def _(distance):
        right.visit_outer(distance, False, wait_send)

    @pl.loop(0, z_size)
    def _(o):
        right.visit_inner(o, False, wait_send)

    @pl.loop(1, col_count)
    def _(d):
        sum_copy(d).wait_send()
        source = (col + d) % col_count
        pltpu.make_async_remote_copy(
            src_ref=sums.at[source],
            dst_ref=sums.at[source],
            send_sem=sum_send.at[d],
            recv_sem=sum_recv.at[source],
            device_id={"col": source},
            device_id_type=MESH,
        ).wait_recv()

    total = sums[0]
    for c in range(1, col_count):
        total = total + sums[c]
    factor = (rows_local * col_count) / total
    for j in range(col_blocks):
        scale[0:1, j * BLOCK:(j + 1) * BLOCK] = factor[j:j + 1, :]


def write_scaled(steps, product, scale, flow, scaled, sem):
    depth = product.shape[0] // steps
    writes = []
    for step in range(steps):
        at = pl.ds(step * depth, depth)
        value = product[at, :]
        scaled[at, :] = value * value * scale[...]
        writes.append(pltpu.make_async_copy(scaled.at[at], flow.at[at], sem.at[step]))
        writes[-1].start()
    for write in writes:
        write.wait()


def shards(row_count, col_count, left_values, left_pattern, right_values, right_pattern):
    rows_local, inner_local = left_values.shape
    inner_rows, cols_local = right_values.shape
    y_size = row_count // 2
    x_size = y_size if col_count % y_size == 0 else 1
    group = inner_local // BLOCK
    left_slots = max(1, group // 2)
    left_blocks = rows_local // BLOCK
    col_blocks = cols_local // BLOCK
    slots = col_blocks // 2
    parts = slots
    inner = row_count * inner_local
    dma = pltpu.SemaphoreType.DMA
    operands = (left_pattern.T, right_pattern, left_values, right_values)
    product, scale = pl.pallas_call(
        functools.partial(kernel, (row_count, col_count, y_size, x_size)),
        out_shape=(
            jax.ShapeDtypeStruct((rows_local, cols_local), jnp.float32),
            jax.ShapeDtypeStruct((1, cols_local), jnp.float32),
        ),
        in_specs=[pl.BlockSpec(memory_space=pltpu.HBM)] * 4,
        out_specs=(pl.BlockSpec(memory_space=pltpu.VMEM),) * 2,
        scratch_shapes=[
            pltpu.SMEM(left_pattern.shape[::-1], jnp.int32),
            pltpu.SMEM(right_pattern.shape, jnp.int32),
            pltpu.VMEM((rows_local, inner_local), jnp.bfloat16),
            pltpu.VMEM((inner_rows, cols_local), jnp.bfloat16),
            pltpu.VMEM((row_count, left_blocks, left_slots, BLOCK, BLOCK), jnp.bfloat16),
            pltpu.VMEM((col_count, slots, BLOCK, BLOCK), jnp.bfloat16),
            pltpu.VMEM((inner // (x_size * BLOCK), rows_local, x_size * BLOCK), jnp.bfloat16),
            pltpu.VMEM((col_count, col_blocks, BLOCK), jnp.float32),
            dma((4,)),
            dma((4, row_count, 1)),
            dma((row_count, 1)),
            dma((4, col_count, parts)),
            dma((col_count, parts)),
            dma((col_count,)),
            dma((col_count,)),
        ],
        compiler_params=pltpu.CompilerParams(
            collective_id=0, has_side_effects=True, vmem_limit_bytes=32 * 1024 * 1024
        ),
    )(*(pltpu.with_memory_space_constraint(x, pltpu.HBM) for x in operands))
    return pl.pallas_call(
        functools.partial(write_scaled, SCALE_STEPS),
        out_shape=jax.ShapeDtypeStruct((rows_local, cols_local), jnp.float32),
        in_specs=[pl.BlockSpec(memory_space=pltpu.VMEM)] * 2,
        out_specs=pl.BlockSpec(memory_space=pltpu.HBM),
        scratch_shapes=[
            pltpu.VMEM((rows_local, cols_local), jnp.float32),
            dma((SCALE_STEPS,)),
        ],
        compiler_params=pltpu.CompilerParams(vmem_limit_bytes=8 * 1024 * 1024),
    )(product, scale)


def solution(mesh):
    return jax.shard_map(
        functools.partial(shards, mesh.shape["row"], mesh.shape["col"]),
        mesh=mesh,
        in_specs=(P("col", "row"), P(), P("col", "row"), P()),
        out_specs=P("col", "row"),
        check_vma=False,
    )
```

```python
import functools

import jax
import jax.numpy as jnp
from jax import lax
from jax.experimental import pallas as pl
from jax.experimental.pallas import tpu as pltpu
from jax.sharding import PartitionSpec as P

BLOCK = 128
SCALE_STEPS = 8
MESH = pl.DeviceIdType.MESH


class Gather:
    def __init__(self, axis, outer, inner, held, send_sem, recv_sem):
        self.axis, self.outer, self.inner = axis, outer, inner
        self.held, self.send_sem, self.recv_sem = held, send_sem, recv_sem
        self.parts = recv_sem.shape[1]
        self.depth = held.shape[1] // self.parts
        me = lax.axis_index(axis)
        self.me, self.o, self.i = me, me // inner, me % inner

    def copy(self, slot, part, lane, target):
        piece = self.held.at[slot, pl.ds(part * self.depth, self.depth)]
        return pltpu.make_async_remote_copy(
            src_ref=piece,
            dst_ref=piece,
            send_sem=self.send_sem.at[lane, slot, part],
            recv_sem=self.recv_sem.at[slot, part],
            device_id={self.axis: target},
            device_id_type=MESH,
        )

    def each_outer(self, slot, part, step, act):
        target = self.o + step

        @pl.when((target >= 0) & (target < self.outer))
        def _():
            act(self.copy(slot, part, 0 if step == 1 else 1, target * self.inner + self.i))

    def each_inner(self, slot, part, step, act):
        target = self.i + step

        @pl.when((target >= 0) & (target < self.inner))
        def _():
            act(self.copy(slot, part, 2 if step == 1 else 3, self.o * self.inner + target))

    def visit_own(self, act):
        for part in range(self.parts):
            for step in (1, -1):
                self.each_outer(self.me, part, step, act)
            for step in (1, -1):
                self.each_inner(self.me, part, step, act)

    def visit_outer(self, distance, wait, act):
        for part in range(self.parts):
            for sign in (-1, 1):
                o = self.o + sign * distance

                @pl.when((o >= 0) & (o < self.outer))
                def _():
                    slot = o * self.inner + self.i
                    if wait:
                        self.copy(slot, part, 0, self.me).wait_recv()
                    self.each_outer(slot, part, -sign, act)
                    for step in (1, -1):
                        self.each_inner(slot, part, step, act)

    def visit_inner(self, o, wait, act):
        for distance in range(1, self.inner):
            for step in (1, -1):
                i = self.i + step * distance

                @pl.when((i >= 0) & (i < self.inner))
                def _():
                    slot = o * self.inner + i
                    for part in range(self.parts):
                        if wait:
                            self.copy(slot, part, 0, self.me).wait_recv()
                        self.each_inner(slot, part, -step, act)

    def greet(self, barrier):
        count = 0
        for step in (1, -1):
            for own, size, stride in ((self.o, self.outer, self.inner), (self.i, self.inner, 1)):
                there = (own + step >= 0) & (own + step < size)

                @pl.when(there)
                def _():
                    pl.semaphore_signal(
                        barrier, inc=1, device_id={self.axis: self.me + step * stride}, device_id_type=MESH
                    )

                count = count + jnp.where(there, 1, 0)
        return count


def start(copy):
    copy.start()


def wait_send(copy):
    copy.wait_send()


def kernel(
    sizes,
    left_ones, right_ones, left_values, right_values,
    product, scale,
    left_pattern, right_pattern, left_in, right_in, left_held, right_held, left_dense, sums,
    in_sem, left_send, left_recv, right_send, right_recv, sum_send, sum_recv,
):
    row_count, col_count, y_size, x_size = sizes
    rows_local, inner_local = left_in.shape
    left_blocks = rows_local // BLOCK
    group = inner_local // BLOCK
    left_slots = left_held.shape[2]
    col_blocks = right_in.shape[1] // BLOCK
    slots = right_held.shape[1]
    z_size = col_count // x_size
    row, col = lax.axis_index("row"), lax.axis_index("col")

    barrier = pltpu.get_barrier_semaphore()

    right = Gather("col", z_size, x_size, right_held, right_send, right_recv)
    left = Gather("row", y_size, row_count // y_size, left_held, left_send, left_recv)
    neighbours = right.greet(barrier) + left.greet(barrier)

    right_load = pltpu.make_async_copy(right_values, right_in, in_sem.at[0])
    left_load = pltpu.make_async_copy(left_values, left_in, in_sem.at[1])
    left_ones_load = pltpu.make_async_copy(left_ones, left_pattern, in_sem.at[2])
    right_ones_load = pltpu.make_async_copy(right_ones, right_pattern, in_sem.at[3])
    left_ones_load.start()
    right_ones_load.start()
    left_load.start()
    right_load.start()

    def pick(ones, wanted, candidate):
        before, found = 0, [None] * wanted
        for k, one in enumerate(ones):
            block = candidate(k)
            for s in range(min(k + 1, wanted)):
                if k == s:
                    found[s] = block
                else:
                    found[s] = jnp.where((one != 0) & (before == s), block, found[s])
            before = before + one
        return found

    def unpick(one, before, packed):
        block = jnp.zeros_like(packed[0])
        for s, value in enumerate(packed):
            block = jnp.where((one != 0) & (before == s), value, block)
        return block

    left_ones_load.wait()
    left_load.wait()
    for b in range(left_blocks):
        ones = [left_pattern[row * group + k, col * left_blocks + b] for k in range(group)]
        at = slice(b * BLOCK, (b + 1) * BLOCK)
        picks = pick(ones, left_slots, lambda k: left_in[at, k * BLOCK:(k + 1) * BLOCK])
        for s in range(left_slots):
            left_held[row, b, s] = picks[s]

    right_ones_load.wait()
    ones = [right_pattern[col, row * col_blocks + j] for j in range(col_blocks)]
    right_load.wait()
    picks = pick(ones, slots, lambda j: right_in[:, j * BLOCK:(j + 1) * BLOCK])
    for s in range(slots):
        right_held[col, s] = picks[s]
    pl.semaphore_wait(barrier, neighbours)
    left.visit_own(start)
    right.visit_own(start)

    product[...] = jnp.zeros_like(product)

    def finish_left():
        @pl.loop(1, y_size)
        def _(distance):
            left.visit_outer(distance, True, start)

        @pl.loop(0, y_size)
        def _(o):
            left.visit_inner(o, True, start)

        @pl.loop(0, row_count * group)
        def _(k):
            g, within = k // group, k % group
            at = pl.ds(pl.multiple_of((k % x_size) * BLOCK, BLOCK), BLOCK)
            for b in range(left_blocks):
                block_row = col * left_blocks + b
                here = left_pattern[k, block_row]
                before = 0
                for m in range(group - 1):
                    before = before + jnp.where(m < within, left_pattern[g * group + m, block_row], 0)
                left_dense[k // x_size, b * BLOCK:(b + 1) * BLOCK, at] = unpick(
                    here, before, [left_held[g, b, s] for s in range(left_slots)]
                )

    def multiply(o):
        right.visit_inner(o, True, start)
        ones, ranks = [], []
        for i in range(x_size):
            k = o * x_size + i
            line = [right_pattern[k, row * col_blocks + j] for j in range(col_blocks)]
            rank = [0] * col_blocks
            for j in range(1, col_blocks):
                rank[j] = rank[j - 1] + line[j - 1]
            ones.append(line)
            ranks.append(rank)

        def dense(i, j):
            packed = [right_held[o * x_size + i, s] for s in range(slots)]
            return unpick(ones[i][j], ranks[i][j], packed)

        for j in range(0, col_blocks, 2):
            block = jnp.concatenate(
                [jnp.concatenate([dense(i, j), dense(i, j + 1)], axis=1) for i in range(x_size)],
                axis=0,
            )
            at = pl.ds(j * BLOCK, 2 * BLOCK)
            product[:, at] += jnp.dot(left_dense[o], block, preferred_element_type=jnp.float32)

    def settle():
        right.visit_own(wait_send)
        left.visit_own(wait_send)

        @pl.loop(1, y_size)
        def _(distance):
            left.visit_outer(distance, False, wait_send)

        @pl.loop(0, y_size)
        def _(o):
            left.visit_inner(o, False, wait_send)

    lag = jnp.where((right.o > 0) & (right.o < z_size - 1), 2, 1)

    @pl.loop(1, z_size + 2)
    def _(t):
        @pl.when(t < z_size)
        def _():
            right.visit_outer(t, True, start)

        @pl.when(t == lag)
        def _():
            finish_left()

        @pl.when(t == 2)
        def _():
            settle()

        @pl.loop(0, 2)
        def _(side):
            distance = t - lag
            o = right.o + (2 * side - 1) * distance

            @pl.when((distance >= 0) & (distance + side > 0) & (o >= 0) & (o < z_size))
            def _():
                multiply(o)

    for j in range(col_blocks):
        part = product[:, j * BLOCK:(j + 1) * BLOCK]
        sums[col, j:j + 1, :] = jnp.sum(part * part, axis=0, keepdims=True)

    def sum_copy(d):
        return pltpu.make_async_remote_copy(
            src_ref=sums.at[col],
            dst_ref=sums.at[col],
            send_sem=sum_send.at[d],
            recv_sem=sum_recv.at[col],
            device_id={"col": (col + d) % col_count},
            device_id_type=MESH,
        )

    @pl.loop(1, col_count)
    def _(d):
        sum_copy(d).start()

    @pl.loop(1, z_size)
    def _(distance):
        right.visit_outer(distance, False, wait_send)

    @pl.loop(0, z_size)
    def _(o):
        right.visit_inner(o, False, wait_send)

    @pl.loop(1, col_count)
    def _(d):
        sum_copy(d).wait_send()
        source = (col + d) % col_count
        pltpu.make_async_remote_copy(
            src_ref=sums.at[source],
            dst_ref=sums.at[source],
            send_sem=sum_send.at[d],
            recv_sem=sum_recv.at[source],
            device_id={"col": source},
            device_id_type=MESH,
        ).wait_recv()

    total = sums[0]
    for c in range(1, col_count):
        total = total + sums[c]
    factor = (rows_local * col_count) / total
    for j in range(col_blocks):
        scale[0:1, j * BLOCK:(j + 1) * BLOCK] = factor[j:j + 1, :]


def write_scaled(steps, product, scale, flow, scaled, sem):
    depth = product.shape[0] // steps
    writes = []
    for step in range(steps):
        at = pl.ds(step * depth, depth)
        value = product[at, :]
        scaled[at, :] = value * value * scale[...]
        writes.append(pltpu.make_async_copy(scaled.at[at], flow.at[at], sem.at[step]))
        writes[-1].start()
    for write in writes:
        write.wait()


def shards(row_count, col_count, left_values, left_pattern, right_values, right_pattern):
    rows_local, inner_local = left_values.shape
    inner_rows, cols_local = right_values.shape
    y_size = row_count // 2
    x_size = y_size if col_count % y_size == 0 else 1
    group = inner_local // BLOCK
    left_slots = max(1, group // 2)
    left_blocks = rows_local // BLOCK
    col_blocks = cols_local // BLOCK
    slots = col_blocks // 2
    parts = 2
    inner = row_count * inner_local
    dma = pltpu.SemaphoreType.DMA
    operands = (left_pattern.T, right_pattern, left_values, right_values)
    product, scale = pl.pallas_call(
        functools.partial(kernel, (row_count, col_count, y_size, x_size)),
        out_shape=(
            jax.ShapeDtypeStruct((rows_local, cols_local), jnp.float32),
            jax.ShapeDtypeStruct((1, cols_local), jnp.float32),
        ),
        in_specs=[pl.BlockSpec(memory_space=pltpu.HBM)] * 4,
        out_specs=(pl.BlockSpec(memory_space=pltpu.VMEM),) * 2,
        scratch_shapes=[
            pltpu.SMEM(left_pattern.shape[::-1], jnp.int32),
            pltpu.SMEM(right_pattern.shape, jnp.int32),
            pltpu.VMEM((rows_local, inner_local), jnp.bfloat16),
            pltpu.VMEM((inner_rows, cols_local), jnp.bfloat16),
            pltpu.VMEM((row_count, left_blocks, left_slots, BLOCK, BLOCK), jnp.bfloat16),
            pltpu.VMEM((col_count, slots, BLOCK, BLOCK), jnp.bfloat16),
            pltpu.VMEM((inner // (x_size * BLOCK), rows_local, x_size * BLOCK), jnp.bfloat16),
            pltpu.VMEM((col_count, col_blocks, BLOCK), jnp.float32),
            dma((4,)),
            dma((4, row_count, 1)),
            dma((row_count, 1)),
            dma((4, col_count, parts)),
            dma((col_count, parts)),
            dma((col_count,)),
            dma((col_count,)),
        ],
        compiler_params=pltpu.CompilerParams(
            collective_id=0, has_side_effects=True, vmem_limit_bytes=32 * 1024 * 1024
        ),
    )(*(pltpu.with_memory_space_constraint(x, pltpu.HBM) for x in operands))
    return pl.pallas_call(
        functools.partial(write_scaled, SCALE_STEPS),
        out_shape=jax.ShapeDtypeStruct((rows_local, cols_local), jnp.float32),
        in_specs=[pl.BlockSpec(memory_space=pltpu.VMEM)] * 2,
        out_specs=pl.BlockSpec(memory_space=pltpu.HBM),
        scratch_shapes=[
            pltpu.VMEM((rows_local, cols_local), jnp.float32),
            dma((SCALE_STEPS,)),
        ],
        compiler_params=pltpu.CompilerParams(vmem_limit_bytes=8 * 1024 * 1024),
    )(product, scale)


def solution(mesh):
    return jax.shard_map(
        functools.partial(shards, mesh.shape["row"], mesh.shape["col"]),
        mesh=mesh,
        in_specs=(P("col", "row"), P(), P("col", "row"), P()),
        out_specs=P("col", "row"),
        check_vma=False,
    )
```
